32 devices in a mesh: dp: 8 (over y, x, core), blk: 4 (over z).
Axes of the slice: x: 2, y: 2, z: 4, core: 2. Of those that a mesh axis runs over, the one named last changes fastest.
Arguments:
- hidden_in: bfloat16 [4, 16, 512, 768], P(None, 'dp', 'blk'), may hold values from -6 to 6
- seq_lengths: int32 [4, 16, 3], P(None, 'dp'), may hold values from 0 to 512, as said below
- dam_mask: int32 [12, 512, 512], replicated, may hold values from 0 to 1, as said below
- w_query: bfloat16 [768, 768], replicated, may hold values from -0.21875 to 0.21875
- b_query: bfloat16 [768], replicated, may hold values from -4 to 4
- w_key: bfloat16 [768, 768], replicated, may hold values from -0.21875 to 0.21875
- w_value: bfloat16 [768, 768], replicated, may hold values from -0.21875 to 0.21875
- b_value: bfloat16 [768], replicated, may hold values from -4 to 4
- w_attn_out: bfloat16 [768, 768], replicated, may hold values from -0.875 to 0.875
- b_attn_out: bfloat16 [768], replicated, may hold values from -4 to 4
- gain_attn: bfloat16 [768], replicated, may hold values from 0.5 to 1.5
- shift_attn: bfloat16 [768], replicated, may hold values from -4 to 4
- w_inner: bfloat16 [768, 3072], replicated, may hold values from -0.21875 to 0.21875
- b_inner: bfloat16 [3072], replicated, may hold values from -4 to 4
- w_outer: bfloat16 [3072, 768], replicated, may hold values from -0.109375 to 0.109375
- b_outer: bfloat16 [768], replicated, may hold values from -4 to 4
- gain_ffn: bfloat16 [768], replicated, may hold values from 0.5 to 1.5
- shift_ffn: bfloat16 [768], replicated, may hold values from -4 to 4
- grad_out: bfloat16 [4, 16, 512, 768], P(None, 'dp', 'blk'), may hold values from -6 to 6
Outputs:
- hidden_out: bfloat16 [4, 16, 512, 768], P(None, 'dp', 'blk')
- grad_in: float32 [4, 16, 512, 768], P(None, 'dp', 'blk')
- grad_w_query: float32 [768, 768], P('dp')
- grad_b_query: float32 [768], P('dp')
- grad_w_key: float32 [768, 768], P('dp')
- grad_w_value: float32 [768, 768], P('dp')
- grad_b_value: float32 [768], P('dp')
- grad_w_attn_out: float32 [768, 768], P('dp')
- grad_b_attn_out: float32 [768], P('dp')
- grad_gain_attn: float32 [768], P('dp')
- grad_shift_attn: float32 [768], P('dp')
- grad_w_inner: float32 [768, 3072], P('dp')
- grad_b_inner: float32 [3072], P('dp')
- grad_w_outer: float32 [3072, 768], P('dp')
- grad_b_outer: float32 [768], P('dp')
- grad_gain_ffn: float32 [768], P('dp')
- grad_shift_ffn: float32 [768], P('dp')
The draws below stay inside these ranges and needn't reach their ends.
Inputs may be any that keep to these rules, and one draw needn't show every extreme that they name: `seq_lengths`: in every packed row the three lengths sum to 512; the row holds one to three sequences whose lengths come first, each 128 or more, and zeros follow. For each index of dp, in one of the 4 micro-batches one of its 2 rows holds a single sequence of 512 tokens. `dam_mask`: entries are 0 or 1; every diagonal entry of every head is 1.
All inputs are finite; a program needn't handle non-finite values.
Results may differ from the reference program's by a relative error of at most 0.018.
Values may be sent and summed in bfloat16 or wider, within the bound.
No kernel may reach another device: no remote copies, remote signals or barrier semaphores. Data moves between devices by JAX's collectives and lax.ppermute only.
A program may use at most 256 MiB of HBM per device.

```python
import jax
import jax.numpy as jnp
from jax import lax

D = 768
HEADS = 12
FF = 3072
SPAN = 512
ROWS = 2
MICRO = 4
PACKS = 16


def draw_seq_lengths(key, part):
    key = jax.random.fold_in(key, 11)
    keys = jax.random.split(key, 6)
    quarter = SPAN // 4
    groups = PACKS // ROWS
    count = jax.random.randint(keys[0], (MICRO, PACKS), 1, 4)
    chosen_row = jax.random.randint(keys[1], (groups,), 0, ROWS)
    chosen_micro = jax.random.randint(keys[5], (groups,), 0, MICRO)
    row_in = jnp.arange(PACKS, dtype=jnp.int32) % ROWS
    group = jnp.arange(PACKS, dtype=jnp.int32) // ROWS
    micro_index = jnp.arange(MICRO, dtype=jnp.int32)
    single = (micro_index[:, None] == chosen_micro[group][None, :]) & (row_in == chosen_row[group])[None, :]
    count = jnp.where(single, 1, count)
    cut_two = jax.random.randint(keys[2], (MICRO, PACKS), quarter, 3 * quarter + 1)
    first = jax.random.randint(keys[3], (MICRO, PACKS), quarter, 2 * quarter + 1)
    extra = jax.random.randint(keys[4], (MICRO, PACKS), 0, 2 * quarter - first + 1)
    second = first + quarter + extra
    zeros = jnp.zeros((MICRO, PACKS), jnp.int32)
    full = jnp.full((MICRO, PACKS), SPAN, jnp.int32)
    one_seq = jnp.stack([full, zeros, zeros], axis=-1)
    two_seq = jnp.stack([cut_two, SPAN - cut_two, zeros], axis=-1)
    three_seq = jnp.stack([first, second - first, SPAN - second], axis=-1)
    picked = jnp.where((count == 1)[..., None], one_seq, jnp.where((count == 2)[..., None], two_seq, three_seq))
    return picked.astype(jnp.int32)


def draw_dam_mask(key, part):
    key = jax.random.fold_in(key, 23)
    keys = jax.random.split(key, 2)
    density = jax.random.randint(keys[0], (HEADS, 1, 1), 10, 60)
    bits = (jax.random.randint(keys[1], (HEADS, SPAN, SPAN), 0, 100) < density).astype(jnp.int32)
    diagonal = jnp.arange(SPAN)[:, None] == jnp.arange(SPAN)[None, :]
    return jnp.where(diagonal[None], 1, bits).astype(jnp.int32)


def strengthened(array, rng, source, target, shards_of, factor):
    owner, partner = [(jnp.arange(array.shape[dim]) // (array.shape[dim] // shards_of)).reshape([-1 if axis == dim else 1 for axis in range(array.ndim)]) for dim in (source, target)]
    chosen = jax.random.permutation(rng, shards_of)[partner]
    strong = (owner == chosen) | (owner == (partner + shards_of // 2) % shards_of)
    return jnp.where(strong, factor * array, array)


def block_levels(key, extent, pieces, least, high):
    level = 1.0
    for dim, blocks in pieces:
        heights = jax.random.uniform(jax.random.fold_in(jax.random.fold_in(key, 6), dim), (blocks,), jnp.float32, least / len(pieces), high / len(pieces))
        level = level * jnp.repeat(jnp.exp(heights), extent[dim] // blocks).reshape((-1,) + (1,) * (len(extent) - 1 - dim))
    return level


def bell_draw(key, dims, scale, bound, pieces=(), kind=jnp.bfloat16):
    array = scale * jax.random.normal(key, dims, jnp.float32)
    if pieces:
        array = array * block_levels(key, dims, pieces, -0.22, 0.18)
    return jnp.clip(array, -bound, bound).astype(kind)


def noise_with(stream_key, dims, scale, bound, cuts, heavy, kind=jnp.bfloat16):
    drawn = scale * jax.random.normal(stream_key, dims, jnp.float32)
    if cuts:
        drawn = drawn * block_levels(stream_key, dims, cuts, -0.22, 0.18)
    return jnp.clip(strengthened(drawn, jax.random.fold_in(stream_key, 3), *heavy), -bound, bound).astype(kind)


def setup_inputs(seed: int = 0) -> dict:
    key_of = jax.random.split(jax.random.key(seed), 20)
    return {
        "hidden_in": bell_draw(key_of[0], (MICRO, PACKS, SPAN, D), 1.0, 6.0, ((1, 8), (2, 4))),
        "seq_lengths": draw_seq_lengths(jax.random.fold_in(key_of[19], 71), 0),
        "dam_mask": draw_dam_mask(jax.random.fold_in(key_of[19], 71), 0),
        "w_query": bell_draw(key_of[3], (D, D), D ** -0.5, 0.21875),
        "b_query": bell_draw(key_of[4], (D,), 0.3, 4.0),
        "w_key": bell_draw(key_of[5], (D, D), D ** -0.5, 0.21875),
        "w_value": bell_draw(key_of[6], (D, D), D ** -0.5, 0.21875),
        "b_value": bell_draw(key_of[7], (D,), 0.3, 4.0),
        "w_attn_out": bell_draw(key_of[8], (D, D), (D // 16) ** -0.5, 0.875),
        "b_attn_out": bell_draw(key_of[9], (D,), 0.3, 4.0),
        "gain_attn": jnp.clip(1.0 + 0.1 * jax.random.normal(key_of[10], (D,), jnp.float32), 0.5, 1.5).astype(jnp.bfloat16),
        "shift_attn": bell_draw(key_of[11], (D,), 0.3, 4.0),
        "w_inner": bell_draw(key_of[12], (D, FF), D ** -0.5, 0.21875),
        "b_inner": bell_draw(key_of[13], (FF,), 0.3, 4.0),
        "w_outer": bell_draw(key_of[14], (FF, D), FF ** -0.5, 0.109375),
        "b_outer": bell_draw(key_of[15], (D,), 0.3, 4.0),
        "gain_ffn": jnp.clip(1.0 + 0.1 * jax.random.normal(key_of[16], (D,), jnp.float32), 0.5, 1.5).astype(jnp.bfloat16),
        "shift_ffn": bell_draw(key_of[17], (D,), 0.3, 4.0),
        "grad_out": noise_with(key_of[18], (MICRO, PACKS, SPAN, D), 1.0, 6.0, ((1, 8), (2, 4)), (1, 3, 8, 2.0)),
    }


EPS = 1e-12
HIGH = lax.Precision.HIGHEST

@jax.custom_vjp
def low(v):
    return lax.optimization_barrier(v.astype(jnp.bfloat16)).astype(jnp.float32)

@jax.custom_vjp
def low_back(v):
    return v

def low_keep(v):
    return (low(v), None)

def low_pass(kept, grad):
    return (grad,)

def back_keep(v):
    return (v, None)

def back_low(kept, grad):
    return (low(grad),)
low.defvjp(low_keep, low_pass)
low_back.defvjp(back_keep, back_low)

def segment_positions(lengths, places):
    first_cut = lengths[:, 0:1]
    second_cut = first_cut + lengths[:, 1:2]
    after_one = (places[None, :] >= first_cut).astype(jnp.int32)
    after_two = (places[None, :] >= second_cut).astype(jnp.int32)
    segment = after_one + after_two
    inside = places[None, :] - after_one * first_cut - after_two * (second_cut - first_cut)
    return (segment, inside)

def layer_norm(values, gain, shift):
    centred = values - lax.optimization_barrier(jnp.mean(values, axis=-1, keepdims=True))
    spread = lax.optimization_barrier(jnp.mean(centred * centred, axis=-1, keepdims=True))
    return centred * lax.rsqrt(spread + EPS) * gain + shift

def project(values, weight):
    return jnp.einsum('rtd,de->rte', values, weight, precision=HIGH)

def layer_rows(tokens, allowed, params):
    w_query, b_query, w_key, w_value, b_value, w_attn_out, b_attn_out, gain_attn, shift_attn, w_inner, b_inner, w_outer, b_outer, gain_ffn, shift_ffn = params
    packs, span, width = tokens.shape
    head_dim = width // HEADS
    queries = low(low_back((project(tokens, w_query) + b_query) * 0.125)).reshape(packs, span, HEADS, head_dim)
    key_rows = low(low_back(project(tokens, w_key))).reshape(packs, span, HEADS, head_dim)
    value_rows = low(low_back(project(tokens, w_value) + b_value)).reshape(packs, span, HEADS, head_dim)
    scores = low_back(jnp.einsum('rqhd,rkhd->rhqk', queries, key_rows, precision=HIGH))
    masked = jnp.where(allowed, scores, -1e+30)
    row_max = lax.optimization_barrier(jnp.max(masked, axis=-1, keepdims=True))
    numerator = jnp.where(allowed, jnp.exp(masked - row_max), 0.0)
    probs_full = numerator / lax.optimization_barrier(jnp.sum(numerator, axis=-1, keepdims=True))
    mixed = jnp.einsum('rhqk,rkhd->rqhd', low(probs_full), value_rows, precision=HIGH).reshape(packs, span, width)
    mixed = low(low_back(mixed))
    attn_branch = low_back(project(mixed, w_attn_out) + b_attn_out)
    first_norm = layer_norm(tokens + attn_branch, gain_attn, shift_attn)
    inner = low_back(project(low(first_norm), w_inner) + b_inner)
    hidden = low(jax.nn.gelu(inner, approximate=False))
    outer = low_back(project(hidden, w_outer) + b_outer)
    return layer_norm(first_norm + outer, gain_ffn, shift_ffn)

def reference(hidden_in, seq_lengths, dam_mask, w_query, b_query, w_key, w_value, b_value, w_attn_out, b_attn_out, gain_attn, shift_attn, w_inner, b_inner, w_outer, b_outer, gain_ffn, shift_ffn, grad_out):
    params = tuple((weight.astype(jnp.float32) for weight in (w_query, b_query, w_key, w_value, b_value, w_attn_out, b_attn_out, gain_attn, shift_attn, w_inner, b_inner, w_outer, b_outer, gain_ffn, shift_ffn)))
    groups = MICRO * PACKS // ROWS
    tokens = hidden_in.astype(jnp.float32).reshape(groups, ROWS, SPAN, D)
    cotangent = grad_out.astype(jnp.float32).reshape(groups, ROWS, SPAN, D)
    lengths = seq_lengths.reshape(groups, ROWS, 3)
    dam = dam_mask == 1
    places = jnp.arange(SPAN, dtype=jnp.int32)

    def lookup(inside):
        return dam[:, inside[:, None], inside[None, :]]

    def one_group(totals, inputs):
        group_tokens, group_cot, group_len = inputs
        segment, inside = segment_positions(group_len, places)
        allowed = (segment[:, :, None] == segment[:, None, :])[:, None] & jax.vmap(lookup)(inside)
        result, pullback = jax.vjp(lambda values, weights: layer_rows(values, allowed, weights), group_tokens, params)
        grad_tokens, grad_params = pullback(group_cot)
        totals = tuple((left + right for left, right in zip(totals, grad_params)))
        return (totals, (result.astype(jnp.bfloat16), grad_tokens))
    zeros = tuple((jnp.zeros_like(weight) for weight in params))
    totals, (outputs, grads_in) = lax.scan(one_group, zeros, (tokens, cotangent, lengths))
    outputs = outputs.reshape(MICRO, PACKS, SPAN, D)
    grads_in = grads_in.reshape(MICRO, PACKS, SPAN, D)
    return (outputs, grads_in, totals[0], totals[1], totals[2], totals[3], totals[4], totals[5], totals[6], totals[7], totals[8], totals[9], totals[10], totals[11], totals[12], totals[13], totals[14])
```

```python
import jax
import jax.numpy as jnp
from jax import lax
from jax.sharding import PartitionSpec as P

HEADS = 12


EPS = 1e-12


def product(left, right):
    return jnp.dot(left, right, preferred_element_type=jnp.float32)


def by_rows(left, right):
    return lax.dot_general(
        left, right, (((0,), (0,)), ((), ())), preferred_element_type=jnp.float32
    )


def by_transpose(left, right):
    return lax.dot_general(
        left, right, (((1,), (1,)), ((), ())), preferred_element_type=jnp.float32
    )


def column_sum(values):
    return jnp.sum(values.astype(jnp.float32), axis=0)


def segment_positions(lengths, places):
    first_cut = lengths[:, 0:1]
    second_cut = first_cut + lengths[:, 1:2]
    after_one = (places[None, :] >= first_cut).astype(jnp.int32)
    after_two = (places[None, :] >= second_cut).astype(jnp.int32)
    segment = after_one + after_two
    inside = places[None, :] - after_one * first_cut - after_two * (second_cut - first_cut)
    return (segment, inside)


def norm_forward(values):
    centred = values - jnp.mean(values, axis=-1, keepdims=True)
    inv_scale = lax.rsqrt(jnp.mean(centred * centred, axis=-1, keepdims=True) + EPS)
    return (centred * inv_scale, inv_scale)


def norm_back(grad_normed, normed, inv_scale):
    mean_grad = jnp.mean(grad_normed, axis=-1, keepdims=True)
    mean_cross = jnp.mean(grad_normed * normed, axis=-1, keepdims=True)
    return inv_scale * (grad_normed - mean_grad - normed * mean_cross)


def swap(values, axis, mask):
    size = lax.axis_size(axis)
    return lax.ppermute(values, axis, [(i, i ^ mask) for i in range(size)])


def scatter_bits(blocks, order):
    size = lax.axis_size("dp")
    bits = size.bit_length() - 1
    place = lax.axis_index("dp")
    held = blocks.reshape((2,) * bits + blocks.shape[1:])
    left = list(range(bits - 1, -1, -1))
    for bit in order:
        axis = left.index(bit)
        mine = (place >> bit) & 1
        keep = lax.dynamic_index_in_dim(held, mine, axis, keepdims=False)
        send = lax.dynamic_index_in_dim(held, 1 - mine, axis, keepdims=False)
        got = swap(send, "dp", 1 << bit)
        held = (keep.astype(jnp.float32) + got.astype(jnp.float32)).astype(jnp.bfloat16)
        left.remove(bit)
    return held


def sum_line(rows):
    size = lax.axis_size("blk")
    bits = size.bit_length() - 1
    place = lax.axis_index("blk")
    held = rows.reshape((2,) * bits + (rows.shape[0] // size,) + rows.shape[1:])
    for bit in range(bits):
        mine = (place >> bit) & 1
        keep = lax.dynamic_index_in_dim(held, mine, 0, keepdims=False)
        send = lax.dynamic_index_in_dim(held, 1 - mine, 0, keepdims=False)
        got = swap(send, "blk", 1 << bit)
        held = (keep.astype(jnp.float32) + got.astype(jnp.float32)).astype(jnp.bfloat16)
    for bit in range(bits - 1, -1, -1):
        mine = (place >> bit) & 1
        got = swap(held, "blk", 1 << bit)
        held = jnp.where(mine == 0, jnp.stack([held, got]), jnp.stack([got, held]))
    return held.reshape(rows.shape)


def local(
    hidden_in,
    seq_lengths,
    dam_mask,
    w_query,
    b_query,
    w_key,
    w_value,
    b_value,
    w_attn_out,
    b_attn_out,
    gain_attn,
    shift_attn,
    w_inner,
    b_inner,
    w_outer,
    b_outer,
    gain_ffn,
    shift_ffn,
    grad_out,
):
    micro, rows, blk_len, width = hidden_in.shape
    head_dim = width // HEADS
    cycle = lax.axis_size("blk")
    groups = lax.axis_size("dp")
    span = blk_len * cycle
    place = lax.axis_index("blk")

    def gather_rows(values):
        parts = []
        for j in range(cycle):
            part = lax.dynamic_index_in_dim(values, place ^ j, 0, keepdims=False)
            if j:
                part = swap(part, "blk", j)
            parts.append(part)
        return jnp.stack(parts, axis=1).reshape(rows * span, width)

    def return_rows(values):
        values = values.reshape(rows, cycle, blk_len, width)
        parts = [values[:, 0]] + [swap(values[:, j], "blk", j) for j in range(1, cycle)]
        stacked = jnp.stack(parts)
        return jnp.take(stacked, jnp.arange(cycle) ^ place, axis=0)

    all_places = jnp.arange(span, dtype=jnp.int32)
    places = ((all_places // blk_len) ^ place) * blk_len + all_places % blk_len
    shifts = jnp.arange(HEADS, dtype=jnp.int32)[:, None, None]
    packed = dam_mask << shifts
    low_bits = jnp.sum(packed[:8], axis=0).astype(jnp.bfloat16)
    high_bits = (jnp.sum(packed[8:], axis=0) >> 8).astype(jnp.bfloat16)

    def gelu_exact(values):
        return jax.nn.gelu(values, approximate=False)

    tokens = gather_rows(hidden_in)
    grad_rows = gather_rows(grad_out).astype(jnp.float32)
    lengths = lax.dynamic_index_in_dim(seq_lengths, place, 0, keepdims=False)
    segment, inside = segment_positions(lengths, places)
    pick = (inside[:, :, None] == all_places).astype(jnp.bfloat16)

    def moved(bits):
        one = jnp.einsum("rtp,pq->rtq", pick, bits, preferred_element_type=jnp.float32)
        two = jnp.einsum(
            "rtq,ruq->rtu", one.astype(jnp.bfloat16), pick, preferred_element_type=jnp.float32
        )
        return two.astype(jnp.int32)

    bits = moved(low_bits) + (moved(high_bits) << 8)
    bits = jnp.where(segment[:, :, None] == segment[:, None, :], bits, 0)
    allowed = ((bits[:, None] >> shifts[None]) & 1) == 1

    queries = ((product(tokens, w_query) + b_query) * 0.125).astype(jnp.bfloat16)
    query_heads = queries.reshape(rows, span, HEADS, head_dim)
    key_heads = product(tokens, w_key).astype(jnp.bfloat16).reshape(rows, span, HEADS, head_dim)
    value_heads = (
        (product(tokens, w_value) + b_value)
        .astype(jnp.bfloat16)
        .reshape(rows, span, HEADS, head_dim)
    )
    scores = jnp.einsum("rqhd,rkhd->rhqk", query_heads, key_heads, preferred_element_type=jnp.float32)
    masked = jnp.where(allowed, scores, -1e30)
    row_max = jnp.max(masked, axis=-1, keepdims=True)
    numerator = jnp.where(allowed, jnp.exp(masked - row_max), 0.0)
    probs_full = numerator / jnp.sum(numerator, axis=-1, keepdims=True)
    probs_low = probs_full.astype(jnp.bfloat16)
    mixed = jnp.einsum("rhqk,rkhd->rqhd", probs_low, value_heads, preferred_element_type=jnp.float32)
    mixed_low = mixed.reshape(rows * span, width).astype(jnp.bfloat16)
    residual_one = tokens.astype(jnp.float32) + product(mixed_low, w_attn_out) + b_attn_out
    normed_one, scale_one = norm_forward(residual_one)
    first_norm = normed_one * gain_attn + shift_attn
    first_low = first_norm.astype(jnp.bfloat16)
    inner = product(first_low, w_inner) + b_inner
    hidden_low = gelu_exact(inner).astype(jnp.bfloat16)
    residual_two = first_norm + product(hidden_low, w_outer) + b_outer
    normed_two, scale_two = norm_forward(residual_two)
    result = normed_two * gain_ffn + shift_ffn
    hidden_out = return_rows(result.astype(jnp.bfloat16))
    d_second = norm_back(grad_rows * gain_ffn, normed_two, scale_two)
    d_outer = d_second.astype(jnp.bfloat16)
    _, gelu_pull = jax.vjp(gelu_exact, inner)
    d_inner = gelu_pull(by_transpose(d_outer, w_outer))[0].astype(jnp.bfloat16)

    def blocks(grad):
        grad = grad.astype(jnp.bfloat16).reshape(groups, -1, grad.shape[1])
        pieces = grad.shape[2] // width
        return [grad[:, :, i * width : (i + 1) * width] for i in range(pieces)]

    early = jnp.concatenate(
        blocks(by_rows(hidden_low, d_outer)) + blocks(by_rows(first_low, d_inner)), axis=1
    )
    early = lax.psum_scatter(early, "dp", scatter_dimension=0, tiled=False)
    early = lax.psum(early, "blk").astype(jnp.float32)

    d_first = d_second + by_transpose(d_inner, w_inner)
    d_residual = norm_back(d_first * gain_attn, normed_one, scale_one)
    d_attn = d_residual.astype(jnp.bfloat16)
    d_mixed = by_transpose(d_attn, w_attn_out).astype(jnp.bfloat16)
    d_mixed_heads = d_mixed.reshape(rows, span, HEADS, head_dim)
    d_probs = jnp.einsum("rqhd,rkhd->rhqk", d_mixed_heads, value_heads, preferred_element_type=jnp.float32)
    d_value_all = jnp.einsum("rhqk,rqhd->rkhd", probs_low, d_mixed_heads, preferred_element_type=jnp.float32)
    d_scores = (
        probs_full * (d_probs - jnp.sum(probs_full * d_probs, axis=-1, keepdims=True))
    ).astype(jnp.bfloat16)
    d_query_sum = jnp.einsum("rhqk,rkhd->rqhd", d_scores, key_heads, preferred_element_type=jnp.float32)
    d_key_all = jnp.einsum("rhqk,rqhd->rkhd", d_scores, query_heads, preferred_element_type=jnp.float32)
    d_keys = d_key_all.reshape(rows * span, width).astype(jnp.bfloat16)
    d_values = d_value_all.reshape(rows * span, width).astype(jnp.bfloat16)
    d_queries = (d_query_sum * 0.125).reshape(rows * span, width).astype(jnp.bfloat16)
    grad_tokens = (
        d_residual
        + by_transpose(d_queries, w_query)
        + by_transpose(d_keys, w_key)
        + by_transpose(d_values, w_value)
    )
    grad_in = return_rows(grad_tokens.astype(jnp.bfloat16)).astype(jnp.float32)

    vectors = [
        column_sum(d_queries),
        column_sum(d_values),
        column_sum(d_attn),
        jnp.sum(d_first * normed_one, axis=0),
        jnp.sum(d_first, axis=0),
        column_sum(d_inner),
        column_sum(d_outer),
        jnp.sum(grad_rows * normed_two, axis=0),
        jnp.sum(grad_rows, axis=0),
    ]
    flat = jnp.concatenate([v.reshape(groups, -1) for v in vectors], axis=1)
    small = flat.shape[1]
    unit = 16 * width
    flat = jnp.pad(flat, ((0, 0), (0, -small % unit)))
    late = jnp.concatenate(
        [
            by_rows(tokens, d_queries).astype(jnp.bfloat16).reshape(groups, -1, width),
            by_rows(tokens, d_keys).astype(jnp.bfloat16).reshape(groups, -1, width),
            by_rows(tokens, d_values).astype(jnp.bfloat16).reshape(groups, -1, width),
            by_rows(mixed_low, d_attn).astype(jnp.bfloat16).reshape(groups, -1, width),
            flat.astype(jnp.bfloat16).reshape(groups, -1, width),
        ],
        axis=1,
    )
    total_bits = groups.bit_length() - 1
    half = late.shape[1] // 2
    first = [0] + list(range(1, total_bits))
    second = [0] + list(range(total_bits - 1, 0, -1))
    late = jnp.concatenate(
        [scatter_bits(late[:, :half], first), scatter_bits(late[:, half:], second)], axis=0
    )
    late = sum_line(late).astype(jnp.float32)

    part = width // groups
    outer_rows = w_outer.shape[0] // groups
    g_outer = early[:outer_rows]
    g_inner = jnp.concatenate(
        [
            early[outer_rows + i * part : outer_rows + (i + 1) * part]
            for i in range(w_inner.shape[1] // width)
        ],
        axis=1,
    )
    g_query, g_key, g_value, g_attn = [late[i * part : (i + 1) * part] for i in range(4)]
    rest = late[4 * part :].reshape(-1)
    small_parts = []
    at = 0
    for v in vectors:
        size = v.shape[0] // groups
        small_parts.append(rest[at : at + size])
        at += size
    s = small_parts
    return (
        hidden_out,
        grad_in,
        g_query,
        s[0],
        g_key,
        g_value,
        s[1],
        g_attn,
        s[2],
        s[3],
        s[4],
        g_inner,
        s[5],
        g_outer,
        s[6],
        s[7],
        s[8],
    )


def solution(mesh):
    placed = (P(None, "dp", "blk", None), P(None, "dp", None)) + (P(),) * 16
    placed = placed + (P(None, "dp", "blk", None),)
    return jax.shard_map(
        local,
        mesh=mesh,
        in_specs=placed,
        out_specs=(
            P(None, "dp", "blk", None),
            P(None, "dp", "blk", None),
            P("dp", None),
            P("dp"),
            P("dp", None),
            P("dp", None),
            P("dp"),
            P("dp", None),
            P("dp"),
            P("dp"),
            P("dp"),
            P("dp", None),
            P("dp"),
            P("dp", None),
            P("dp"),
            P("dp"),
            P("dp"),
        ),
        check_vma=False,
    )
```

```python
import functools

import jax
import jax.numpy as jnp
from jax import lax
from jax.experimental import pallas as pl
from jax.experimental.pallas import tpu as pltpu
from jax.sharding import PartitionSpec as P

HEADS = 12


EPS = 1e-12
F32 = jnp.float32
BF16 = jnp.bfloat16
NN = ((1,), (0,))
NT = ((1,), (1,))
LIMIT = 56 * 1024 * 1024
GROUP = 4
LANES = 128


def dot(left, right, dims=NN):
    return lax.dot_general(left, right, (dims, ((), ())), preferred_element_type=F32)


def params():
    return pltpu.CompilerParams(vmem_limit_bytes=LIMIT)


def cost(flops, moved):
    return pl.CostEstimate(flops=int(flops), bytes_accessed=int(moved), transcendentals=0)


def whole(shape):
    return pl.BlockSpec(shape, lambda *_: (0,) * len(shape))


def once(shape):
    return pl.BlockSpec(shape, lambda *_: (0,) * len(shape), pipeline_mode=pl.Buffered(1))


SMEM = pl.BlockSpec(memory_space=pltpu.SMEM)


def mask_kernel(blk_len, place_ref, len_ref, dam_ref, bits_ref, low_ref, high_ref):
    step = pl.program_id(0)
    chunk = dam_ref.shape[1]
    span = dam_ref.shape[2]
    rows = bits_ref.shape[0]
    low = dam_ref[0]
    for h in range(1, 8):
        low = low + (dam_ref[h] << h)
    high = dam_ref[8]
    for h in range(9, HEADS):
        high = high + (dam_ref[h] << (h - 8))
    at = pl.ds(pl.multiple_of(step * chunk, chunk), chunk)
    low_ref[at, :] = low.astype(F32).astype(BF16)
    high_ref[at, :] = high.astype(F32).astype(BF16)

    @pl.when(step == pl.num_programs(0) - 1)
    def _():
        place = place_ref[0]

        def places(axis):
            local = lax.broadcasted_iota(jnp.int32, (span, span), axis)
            return (((local // blk_len) ^ place) * blk_len) + local % blk_len

        for r in range(rows):
            first = len_ref[r, 0]
            second = first + len_ref[r, 1]

            def segment(at_place):
                one = jnp.where(at_place >= first, 1, 0)
                return one + jnp.where(at_place >= second, 1, 0)

            down = places(0)
            inside = (
                down
                - jnp.where(down >= first, first, 0)
                - jnp.where(down >= second, second - first, 0)
            )
            across = lax.broadcasted_iota(jnp.int32, (span, span), 1)
            pick = jnp.where(inside == across, 1.0, 0.0).astype(BF16)

            def moved(table):
                one = dot(pick, table, NT).astype(BF16)
                return dot(one, pick, NT).astype(jnp.int32)

            bits = moved(low_ref[...]) + (moved(high_ref[...]) << 8)
            bits_ref[r] = jnp.where(segment(down) == segment(places(1)), bits, 0)


def mask_bits(place, lengths, dam_mask, blk_len):
    heads, span, _ = dam_mask.shape
    rows = lengths.shape[0]
    chunk = 64
    return pl.pallas_call(
        functools.partial(mask_kernel, blk_len),
        grid=(span // chunk,),
        in_specs=[SMEM, SMEM, pl.BlockSpec((heads, chunk, span), lambda i: (0, i, 0))],
        out_specs=whole((rows, span, span)),
        out_shape=jax.ShapeDtypeStruct((rows, span, span), jnp.int32),
        scratch_shapes=[pltpu.VMEM((span, span), BF16)] * 2,
        compiler_params=params(),
        cost_estimate=cost(8 * span**3, 4 * heads * span * span),
        name="mask_bits",
    )(place.reshape(1), lengths, dam_mask)


def attn_kernel(cycle, *refs):
    pieces = refs[:cycle]
    wq, wk, wv, bq, bv, bits_ref = refs[cycle : cycle + 6]
    q_out, k_out, v_out, e_out, inv_out, mix_t_out, mix_out, x_out, x_t_out, x_s = refs[cycle + 6 :]
    step = pl.program_id(0)
    blk_len = pieces[0].shape[0]
    span = x_s.shape[0]
    wide = wq.shape[1]

    @pl.when(step == 0)
    def _():
        for j in range(cycle):
            x_s[j * blk_len : (j + 1) * blk_len, :] = pieces[j][...]

    x = x_s[...]
    cols = pl.ds(pl.multiple_of(step * wide, wide), wide)
    x_cols = x_s[:, cols]
    x_out[...] = x_cols
    x_t_out[...] = x_cols.T
    q4 = ((dot(x, wq[...]) + bq[...].astype(F32)) * 0.125).astype(BF16)
    k4 = dot(x, wk[...])
    v4 = (dot(x, wv[...]) + bv[...].astype(F32)).astype(BF16)
    q_out[...] = q4
    k_out[...] = k4.astype(BF16)
    v_out[...] = v4
    v_t = v4.T
    lane = lax.broadcasted_iota(jnp.int32, (span, LANES), 1)
    ones = jnp.ones((16, span), BF16)
    half = span // 2
    for i in range(GROUP):
        pair, side = i // 2, i % 2
        k_pair = k4[:, pair * LANES : (pair + 1) * LANES]
        k_head = jnp.where((lane >= 64) == (side == 1), k_pair, 0.0).astype(BF16)
        bit = jnp.left_shift(jnp.int32(1), GROUP * step + i)
        for part in range(2):
            at = slice(part * half, (part + 1) * half)
            s = dot(k_head, q4[at, pair * LANES : (pair + 1) * LANES], NT)
            s = jnp.where((bits_ref[0, :, at] & bit) != 0, s, -1e30)
            top = jnp.max(s, axis=0, keepdims=True)
            e_out[i, :, at] = jnp.exp(s - top).astype(BF16)
        left = jnp.concatenate([v_t[64 * i : 64 * (i + 1), :], ones], axis=0)
        both = dot(left, e_out[i])
        inv = 1.0 / both[64:65, :]
        inv_out[0, i : i + 1, :] = inv
        mix_t_out[64 * i : 64 * (i + 1), :] = (both[:64, :] * inv).astype(BF16)
    mix_out[...] = mix_t_out[...].T


def attn_forward(pieces, w_query, w_key, w_value, b_query, b_value, bits, row):
    cycle = len(pieces)
    blk_len, width = pieces[0].shape
    span = blk_len * cycle
    wide = 64 * GROUP
    steps = width // wide
    col = pl.BlockSpec((span, wide), lambda g: (0, g))
    col_t = pl.BlockSpec((wide, span), lambda g: (g, 0))
    weight = pl.BlockSpec((width, wide), lambda g: (0, g))
    bias = pl.BlockSpec((1, wide), lambda g: (0, g))
    token = jax.ShapeDtypeStruct((span, width), BF16)
    token_t = jax.ShapeDtypeStruct((width, span), BF16)
    return pl.pallas_call(
        functools.partial(attn_kernel, cycle),
        grid=(steps,),
        in_specs=[once((blk_len, width))] * cycle
        + [weight] * 3
        + [bias] * 2
        + [pl.BlockSpec((1, span, span), lambda g: (row, 0, 0), pipeline_mode=pl.Buffered(1))],
        out_specs=[
            col,
            col,
            col,
            pl.BlockSpec((GROUP, span, span), lambda g: (g, 0, 0)),
            pl.BlockSpec((1, 8, span), lambda g: (g, 0, 0)),
            col_t,
            col,
            col,
            col_t,
        ],
        out_shape=[
            token,
            token,
            token,
            jax.ShapeDtypeStruct((HEADS, span, span), BF16),
            jax.ShapeDtypeStruct((steps, 8, span), F32),
            token_t,
            token,
            token,
            token_t,
        ],
        scratch_shapes=[pltpu.VMEM((span, width), BF16)],
        compiler_params=params(),
        cost_estimate=cost(6 * span * width * width + 8 * 2 * 128 * HEADS * span * span, 16e6),
        name="attn_forward",
    )(*pieces, w_query, w_key, w_value, b_query, b_value, bits)


def norm_forward(values):
    centred = values - jnp.mean(values, axis=-1, keepdims=True)
    inv_scale = lax.rsqrt(jnp.mean(centred * centred, axis=-1, keepdims=True) + EPS)
    return (centred * inv_scale, inv_scale)


def norm_back(grad_normed, normed, inv_scale):
    mean_grad = jnp.mean(grad_normed, axis=-1, keepdims=True)
    mean_cross = jnp.mean(grad_normed * normed, axis=-1, keepdims=True)
    return inv_scale * (grad_normed - mean_grad - normed * mean_cross)


def gelu_parts(values):
    cdf = 0.5 + 0.5 * lax.erf(values * 0.7071067811865476)
    slope = cdf + values * (jnp.exp(-0.5 * values * values) * 0.3989422804014327)
    return values * cdf, slope


def total(values):
    return jnp.sum(values, axis=0, keepdims=True)


def ffn_kernel(cycle, *refs):
    grads = refs[:cycle]
    (x_ref, mix_ref, w_o, w_in, w_out, b_o, gain1, shift1, b_in, b_out, gain2, shift2) = refs[
        cycle : cycle + 12
    ]
    (vec_in, wide_in) = refs[cycle + 12 : cycle + 14]
    outs = refs[cycle + 14 :]
    h_out = outs[:cycle]
    (
        first_t_out,
        hidden_out,
        d_inner_out,
        d_outer_t_out,
        d_attn_out,
        d_res_out,
        d_mix_t_out,
        vec_out,
        wide_out,
        wo_s,
        win_s,
        wout_s,
        slope_s,
        g_s,
        sems,
    ) = outs[cycle:]
    copies = [
        pltpu.make_async_copy(src, dst, sems.at[i])
        for i, (src, dst) in enumerate(((w_o, wo_s), (w_in, win_s), (w_out, wout_s)))
    ]
    for copy in copies:
        copy.start()
    blk_len, width = grads[0].shape
    inner_width = win_s.shape[1]
    for j in range(cycle):
        g_s[j * blk_len : (j + 1) * blk_len, :] = grads[j][...]
    copies[0].wait()
    residual = x_ref[...].astype(F32) + dot(mix_ref[...], wo_s[...]) + b_o[...].astype(F32)
    normed_one, scale_one = norm_forward(residual)
    first = normed_one * gain1[...].astype(F32) + shift1[...].astype(F32)
    first_low = first.astype(BF16)
    first_t_out[...] = first_low.T
    copies[1].wait()
    chunks = [slice(i * width, (i + 1) * width) for i in range(inner_width // width)]
    for at in chunks:
        inner = dot(first_low, win_s[:, at]) + b_in[:, at].astype(F32)
        hidden, slope = gelu_parts(inner)
        hidden_out[:, at] = hidden.astype(BF16)
        slope_s[:, at] = slope.astype(BF16)
    copies[2].wait()
    second = first + dot(hidden_out[...], wout_s[...]) + b_out[...].astype(F32)
    normed_two, scale_two = norm_forward(second)
    result = (normed_two * gain2[...].astype(F32) + shift2[...].astype(F32)).astype(BF16)
    for j in range(cycle):
        h_out[j][...] = result[j * blk_len : (j + 1) * blk_len, :]
    grad = g_s[...].astype(F32)
    vec_out[4:5, :] = vec_in[4:5, :] + total(grad * normed_two)
    vec_out[5:6, :] = vec_in[5:6, :] + total(grad)
    d_second = norm_back(grad * gain2[...].astype(F32), normed_two, scale_two)
    d_outer = d_second.astype(BF16)
    d_outer_t_out[...] = d_outer.T
    vec_out[3:4, :] = vec_in[3:4, :] + total(d_outer.astype(F32))
    for at in chunks:
        d_hidden = dot(d_outer, wout_s[at, :], NT)
        d_inner = (d_hidden * slope_s[:, at].astype(F32)).astype(BF16)
        d_inner_out[:, at] = d_inner
        wide_out[0:1, at] = wide_in[0:1, at] + total(d_inner.astype(F32))
    d_first = d_second + dot(d_inner_out[...], win_s[...], NT)
    vec_out[1:2, :] = vec_in[1:2, :] + total(d_first * normed_one)
    vec_out[2:3, :] = vec_in[2:3, :] + total(d_first)
    d_res = norm_back(d_first * gain1[...].astype(F32), normed_one, scale_one)
    d_res_out[...] = d_res
    d_attn = d_res.astype(BF16)
    d_attn_out[...] = d_attn
    vec_out[0:1, :] = vec_in[0:1, :] + total(d_attn.astype(F32))
    d_mix_t_out[...] = dot(wo_s[...], d_attn, NT).astype(BF16)


def ffn_both(grads, x, mixed, weights, vectors, vec_in, wide_in):
    cycle = len(grads)
    span, width = x.shape
    blk_len = span // cycle
    inner_width = weights[1].shape[1]
    token = jax.ShapeDtypeStruct((span, width), BF16)
    token_t = jax.ShapeDtypeStruct((width, span), BF16)
    wide = jax.ShapeDtypeStruct((span, inner_width), BF16)
    out_shape = [jax.ShapeDtypeStruct((blk_len, width), BF16)] * cycle + [
        token_t,
        wide,
        wide,
        token_t,
        token,
        jax.ShapeDtypeStruct((span, width), F32),
        token_t,
        jax.ShapeDtypeStruct((8, width), F32),
        jax.ShapeDtypeStruct((8, inner_width), F32),
    ]
    vmem = pl.BlockSpec(memory_space=pltpu.VMEM)
    return pl.pallas_call(
        functools.partial(ffn_kernel, cycle),
        in_specs=[vmem] * (cycle + 2)
        + [pl.BlockSpec(memory_space=pl.ANY)] * 3
        + [vmem] * (len(vectors) + 2),
        out_specs=[vmem] * len(out_shape),
        out_shape=out_shape,
        scratch_shapes=[
            pltpu.VMEM(weights[0].shape, BF16),
            pltpu.VMEM(weights[1].shape, BF16),
            pltpu.VMEM(weights[2].shape, BF16),
            pltpu.VMEM((span, inner_width), BF16),
            pltpu.VMEM((span, width), BF16),
            pltpu.SemaphoreType.DMA((3,)),
        ],
        compiler_params=params(),
        cost_estimate=cost(
            2 * span * width * (2 * width + 4 * inner_width), 2 * (2 * inner_width * width) + 16e6
        ),
        name="ffn_both",
    )(*grads, x, mixed, *weights, *vectors, vec_in, wide_in)


def place_parts(tile_ref, my, keep_ref, send_ref, part, put):
    groups = tile_ref.shape[0] // part
    for p in range(groups):
        at = pl.ds(pl.multiple_of((my ^ p) * part, 16), part)
        put(send_ref if p % 2 else keep_ref, p // 2, tile_ref[at, :])


def ffn_grad_kernel(
    my_ref,
    dot0,
    dot1,
    hid0,
    hid1,
    ft0,
    ft1,
    din0,
    din1,
    keep_o,
    send_o,
    keep_i,
    send_i,
    tile_s,
):
    my = my_ref[0]
    outer = (dot(dot0[...], hid0[...]) + dot(dot1[...], hid1[...])).astype(BF16)
    half = outer.shape[1] // 2

    @pl.when(my % 2 == 0)
    def _():
        keep_o[0] = outer[:, :half]
        send_o[0] = outer[:, half:]

    @pl.when(my % 2 == 1)
    def _():
        send_o[0] = outer[:, :half]
        keep_o[0] = outer[:, half:]

    tile_s[...] = (dot(ft0[...], din0[...]) + dot(ft1[...], din1[...])).astype(BF16)

    def put(ref, at, value):
        ref[at, 0] = value

    place_parts(tile_s, my, keep_i, send_i, keep_i.shape[2], put)


def ffn_grads_split(my, d_outer_t, hidden, first_t, d_inner, groups):
    width, span = d_outer_t[0].shape
    inner_width = hidden[0].shape[1]
    part = width // groups
    steps = inner_width // width
    half = width // 2
    lhs = pl.BlockSpec((width, span), lambda i, m: (0, 0), pipeline_mode=pl.Buffered(1))
    moved = pl.BlockSpec((span, width), lambda i, m: (0, (m[0] // 2) ^ i))
    plain = pl.BlockSpec((span, width), lambda i, m: (0, i))
    outer = jax.ShapeDtypeStruct((steps, width, half), BF16)
    inner = jax.ShapeDtypeStruct((groups // 2, steps, part, width), BF16)
    return pl.pallas_call(
        ffn_grad_kernel,
        grid_spec=pltpu.PrefetchScalarGridSpec(
            num_scalar_prefetch=1,
            grid=(steps,),
            in_specs=[lhs, lhs, moved, moved, lhs, lhs, plain, plain],
            out_specs=[pl.BlockSpec((1, width, half), lambda i, m: (i, 0, 0))] * 2
            + [pl.BlockSpec((groups // 2, 1, part, width), lambda i, m: (0, i, 0, 0))] * 2,
            scratch_shapes=[pltpu.VMEM((width, width), BF16)],
        ),
        out_shape=[outer, outer, inner, inner],
        compiler_params=params(),
        cost_estimate=cost(8 * span * width * inner_width, 24e6),
        name="ffn_grads",
    )(my.reshape(1), *d_outer_t, *hidden, *first_t, *d_inner)


def pair_product_kernel(a0, a1, b0, b1, out):
    out[...] = (dot(a0[...], b0[...]) + dot(a1[...], b1[...])).astype(BF16)


def pair_product(left, right):
    depth = left[0].shape[1]
    rows = left[0].shape[0]
    columns = right[0].shape[1]
    wide = 768
    lhs = pl.BlockSpec((rows, depth), lambda i: (0, 0))
    rhs = pl.BlockSpec((depth, wide), lambda i: (0, i))
    return pl.pallas_call(
        pair_product_kernel,
        grid=(columns // wide,),
        in_specs=[lhs, lhs, rhs, rhs],
        out_specs=pl.BlockSpec((rows, wide), lambda i: (0, i)),
        out_shape=jax.ShapeDtypeStruct((rows, columns), BF16),
        compiler_params=params(),
        cost_estimate=cost(4 * rows * columns * depth, 16e6),
        name="pair_product",
    )(*left, *right)


def attn_back_kernel(cycle, *refs):
    (q_ref, k_ref, v_ref, e_ref, inv_ref, mix_t, d_mix_t, wq, wk, wv, d_res, vec_in) = refs[:12]
    g_out = refs[12 : 12 + cycle]
    dq_out, dk_out, dv_out, vec_out, acc, dq_t = refs[12 + cycle :]
    step = pl.program_id(0)
    span = q_ref.shape[0]
    blk_len = span // cycle
    k_t = k_ref[...].T
    lane = lax.broadcasted_iota(jnp.int32, (span, LANES), 1)
    blank = jnp.zeros((64, span), BF16)
    for pair in range(GROUP // 2):
        at = slice(pair * LANES, (pair + 1) * LANES)
        q_pair = q_ref[:, at]
        v_pair = v_ref[:, at]
        d_keys = []
        d_values = None
        for side in range(2):
            i = 2 * pair + side
            mine = slice(64 * i, 64 * (i + 1))
            scaled = d_mix_t[mine, :].astype(F32) * inv_ref[0, i : i + 1, :]
            cross = jnp.sum(scaled * mix_t[mine, :].astype(F32), axis=0, keepdims=True)
            scaled = scaled.astype(BF16)
            padded = jnp.concatenate([blank, scaled] if side else [scaled, blank], axis=0)
            d_probs = dot(v_pair, padded)
            d_scores = (e_ref[i].astype(F32) * (d_probs - cross)).astype(BF16)
            d_keys.append(dot(d_scores, q_pair))
            d_value = dot(e_ref[i], padded, NT)
            d_values = d_value if d_values is None else d_values + d_value
            dq_t[mine, :] = dot(k_t[mine, :], d_scores)
        dk_out[:, at] = jnp.where(lane >= 64, d_keys[1], d_keys[0]).astype(BF16)
        dv_out[:, at] = d_values.astype(BF16)
    dq_out[...] = (dq_t[...] * 0.125).T.astype(BF16)
    vec_out[...] = vec_in[...]
    vec_out[0:1, :] += total(dq_out[...].astype(F32))
    vec_out[1:2, :] += total(dv_out[...].astype(F32))
    more = dot(dq_out[...], wq[...], NT) + dot(dk_out[...], wk[...], NT)
    more = more + dot(dv_out[...], wv[...], NT)

    @pl.when(step == 0)
    def _():
        acc[...] = d_res[...] + more

    @pl.when(step > 0)
    def _():
        acc[...] += more

    @pl.when(step == pl.num_programs(0) - 1)
    def _():
        for j in range(cycle):
            g_out[j][...] = acc[j * blk_len : (j + 1) * blk_len, :].astype(BF16)


def attn_back(cycle, q, k, v, e, inv, mix_t, d_mix_t, w_query, w_key, w_value, d_res, vec_in):
    span, width = q.shape
    blk_len = span // cycle
    wide = 64 * GROUP
    steps = width // wide
    col = pl.BlockSpec((span, wide), lambda g: (0, g))
    col_t = pl.BlockSpec((wide, span), lambda g: (g, 0))
    weight = pl.BlockSpec((width, wide), lambda g: (0, g))
    small = pl.BlockSpec((8, wide), lambda g: (0, g))
    token = jax.ShapeDtypeStruct((span, width), BF16)
    return pl.pallas_call(
        functools.partial(attn_back_kernel, cycle),
        grid=(steps,),
        in_specs=[
            col,
            col,
            col,
            pl.BlockSpec((GROUP, span, span), lambda g: (g, 0, 0)),
            pl.BlockSpec((1, 8, span), lambda g: (g, 0, 0)),
            col_t,
            col_t,
            weight,
            weight,
            weight,
            once((span, width)),
            small,
        ],
        out_specs=[whole((blk_len, width))] * cycle + [col] * 3 + [small],
        out_shape=[jax.ShapeDtypeStruct((blk_len, width), BF16)] * cycle
        + [token] * 3
        + [jax.ShapeDtypeStruct((8, width), F32)],
        scratch_shapes=[pltpu.VMEM((span, width), F32), pltpu.VMEM((wide, span), F32)],
        compiler_params=params(),
        cost_estimate=cost(6 * span * width * width + 16 * 2 * 128 * HEADS * span * span, 16e6),
        name="attn_back",
    )(q, k, v, e, inv, mix_t, d_mix_t, w_query, w_key, w_value, d_res, vec_in)


def attn_grad_kernel(my_ref, xt0, xt1, dq0, dq1, dk0, dk1, dv0, dv1, mt0, mt1, da0, da1, vec, keep, send, tile_s):
    my = my_ref[0]
    part = tile_s.shape[0] // (2 * keep.shape[0])
    work = (
        (xt0, dq0, xt1, dq1),
        (xt0, dk0, xt1, dk1),
        (xt0, dv0, xt1, dv1),
        (mt0, da0, mt1, da1),
    )
    for w, (a0, b0, a1, b1) in enumerate(work):
        tile_s[...] = (dot(a0[...], b0[...]) + dot(a1[...], b1[...])).astype(BF16)

        def put(ref, at, value):
            ref[at, w * part : (w + 1) * part, :] = value

        place_parts(tile_s, my, keep, send, part, put)
    low = vec[...].astype(BF16)
    for p in range(keep.shape[0]):
        keep[p, 4 * part :, :] = low
        send[p, 4 * part :, :] = low


def attn_grads_split(my, x_t, d_queries, d_keys, d_values, mix_t, d_attn, vec, groups):
    width, span = x_t[0].shape
    part = width // groups
    vmem = pl.BlockSpec(memory_space=pltpu.VMEM)
    shape = jax.ShapeDtypeStruct((groups // 2, 4 * part + 32, width), BF16)
    return pl.pallas_call(
        attn_grad_kernel,
        in_specs=[SMEM] + [vmem] * 13,
        out_specs=[vmem] * 2,
        out_shape=[shape] * 2,
        scratch_shapes=[pltpu.VMEM((width, width), BF16)],
        compiler_params=params(),
        cost_estimate=cost(16 * span * width * width, 16e6),
        name="attn_grads",
    )(my.reshape(1), *x_t, *d_queries, *d_keys, *d_values, *mix_t, *d_attn, vec)


def swap(values, axis, mask):
    size = lax.axis_size(axis)
    return lax.ppermute(values, axis, [(i, i ^ mask) for i in range(size)])


def added(left, right):
    return (left.astype(F32) + right.astype(F32)).astype(BF16)


def scatter_rest(keep, got, bits):
    held = added(keep, got)
    for at, bit in enumerate(bits):
        rest = bits[at + 1 :]
        size = held.shape[0]
        alive = [0]
        for other in sorted([bit] + rest):
            alive = alive + [p | (1 << (other - 1)) for p in alive]
        keep_at = [n for n, p in enumerate(alive) if not (p >> (bit - 1)) & 1]
        send_at = [n for n, p in enumerate(alive) if (p >> (bit - 1)) & 1]
        assert size == len(alive)
        send = jnp.stack([held[n] for n in send_at])
        keep = jnp.stack([held[n] for n in keep_at])
        got = swap(send, "dp", 1 << bit)
        held = added(keep, got)
    return held[0]


def scatter_bits(blocks, order):
    size = lax.axis_size("dp")
    bits = size.bit_length() - 1
    place = lax.axis_index("dp")
    held = blocks.reshape((2,) * bits + blocks.shape[1:])
    left = list(range(bits - 1, -1, -1))
    for bit in order:
        axis = left.index(bit)
        mine = (place >> bit) & 1
        keep = lax.dynamic_index_in_dim(held, mine, axis, keepdims=False)
        send = lax.dynamic_index_in_dim(held, 1 - mine, axis, keepdims=False)
        held = added(keep, swap(send, "dp", 1 << bit))
        left.remove(bit)
    return held


def sum_line(rows):
    size = lax.axis_size("blk")
    bits = size.bit_length() - 1
    place = lax.axis_index("blk")
    held = rows.reshape((2,) * bits + (rows.shape[0] // size,) + rows.shape[1:])
    for bit in range(bits):
        mine = (place >> bit) & 1
        keep = lax.dynamic_index_in_dim(held, mine, 0, keepdims=False)
        send = lax.dynamic_index_in_dim(held, 1 - mine, 0, keepdims=False)
        held = added(keep, swap(send, "blk", 1 << bit))
    for bit in range(bits - 1, -1, -1):
        mine = (place >> bit) & 1
        got = swap(held, "blk", 1 << bit)
        held = jnp.where(mine == 0, jnp.stack([held, got]), jnp.stack([got, held]))
    return held.reshape(rows.shape)


def late_kernel(lanes_ref, late, *outs):
    part = outs[0].shape[0]
    for w in range(4):
        outs[w][...] = late[w * part : (w + 1) * part, :].astype(F32)
    vec = late[4 * part :, :]
    width = vec.shape[1]
    size = outs[4].shape[1]

    def picked(start, count):
        lanes = -(-count // LANES) * LANES
        source = lax.broadcasted_iota(jnp.int32, (width, lanes), 0)
        target = lax.broadcasted_iota(jnp.int32, (width, lanes), 1)
        return jnp.where(source == target + start, 1.0, 0.0).astype(BF16)

    narrow = dot(vec, picked(lanes_ref[0], size))
    for n in range(8):
        outs[4 + n][...] = narrow[n : n + 1, :size]
    count = outs[12].shape[1]
    broad = dot(vec, picked(lanes_ref[1], count))
    row = lax.broadcasted_iota(jnp.int32, broad.shape, 0)
    broad = jnp.where(row == lanes_ref[2], broad, 0.0)
    outs[12][...] = total(broad)[:, :count]


def late_results(late, groups, inner_width):
    width = late.shape[1]
    part = (late.shape[0] - 32) // 4
    size = width // groups
    count = inner_width // groups
    my = lax.axis_index("dp")
    start = my * count
    lanes = jnp.stack([my * size, start % width, 8 + start // width]).astype(jnp.int32)
    vmem = pl.BlockSpec(memory_space=pltpu.VMEM)
    shapes = (
        [jax.ShapeDtypeStruct((part, width), F32)] * 4
        + [jax.ShapeDtypeStruct((1, size), F32)] * 8
        + [jax.ShapeDtypeStruct((1, count), F32)]
    )
    outs = pl.pallas_call(
        late_kernel,
        in_specs=[SMEM, vmem],
        out_specs=[vmem] * len(shapes),
        out_shape=shapes,
        compiler_params=params(),
        cost_estimate=cost(1e6, 3e6),
        name="late_results",
    )(lanes, late)
    return list(outs[:4]), [value.reshape(-1) for value in outs[4:]]


def spread_kernel(cycle, rows, place_ref, *refs):
    pieces = refs[:-1]
    out = refs[-1]
    for r in range(rows):
        for j in range(cycle):
            out[place_ref[0] ^ j, r] = pieces[r * cycle + j][...].astype(out.dtype)


def spread(place, pieces, dtype):
    rows, cycle = len(pieces), len(pieces[0])
    blk_len, width = pieces[0][0].shape
    vmem = pl.BlockSpec(memory_space=pltpu.VMEM)
    return pl.pallas_call(
        functools.partial(spread_kernel, cycle, rows),
        in_specs=[SMEM] + [vmem] * (rows * cycle),
        out_specs=vmem,
        out_shape=jax.ShapeDtypeStruct((cycle, rows, blk_len, width), dtype),
        compiler_params=params(),
        cost_estimate=cost(1e6, 5e6),
        name="spread",
    )(place.reshape(1), *[piece for row in pieces for piece in row])


def local(
    hidden_in,
    seq_lengths,
    dam_mask,
    w_query,
    b_query,
    w_key,
    w_value,
    b_value,
    w_attn_out,
    b_attn_out,
    gain_attn,
    shift_attn,
    w_inner,
    b_inner,
    w_outer,
    b_outer,
    gain_ffn,
    shift_ffn,
    grad_out,
):
    micro, rows, blk_len, width = hidden_in.shape
    cycle = lax.axis_size("blk")
    groups = lax.axis_size("dp")
    inner_width = w_inner.shape[1]
    place = lax.axis_index("blk")
    my = lax.axis_index("dp")

    def gather_row(values, row):
        mine = values[:, row]
        parts = [lax.dynamic_index_in_dim(mine, place ^ j, 0, keepdims=False) for j in range(cycle)]
        return [parts[0]] + [swap(parts[j], "blk", j) for j in range(1, cycle)]

    def return_row(parts):
        return [parts[0]] + [swap(parts[j], "blk", j) for j in range(1, cycle)]

    def flat(vector):
        return vector.reshape(1, -1)

    tokens = [gather_row(hidden_in, r) for r in range(rows)]
    grads = [gather_row(grad_out, r) for r in range(rows)]
    lengths = lax.dynamic_index_in_dim(seq_lengths, place, 0, keepdims=False)
    bits = mask_bits(place, lengths, dam_mask, blk_len)
    vectors = [
        flat(v)
        for v in (b_attn_out, gain_attn, shift_attn, b_inner, b_outer, gain_ffn, shift_ffn)
    ]
    vec = jnp.zeros((8, width), F32)
    wide = jnp.zeros((8, inner_width), F32)
    kept = []
    results = []
    for r in range(rows):
        ahead = attn_forward(
            tokens[r], w_query, w_key, w_value, flat(b_query), flat(b_value), bits, r
        )
        x, mixed = ahead[7], ahead[6]
        after = ffn_both(
            grads[r], x, mixed, (w_attn_out, w_inner, w_outer), vectors, vec, wide
        )
        results.append(return_row(after[:cycle]))
        vec, wide = after[-2:]
        kept.append((ahead, after[cycle:-2]))
    hidden_out = spread(place, results, BF16)

    first_t = [k[1][0] for k in kept]
    hidden = [k[1][1] for k in kept]
    d_inner = [k[1][2] for k in kept]
    d_outer_t = [k[1][3] for k in kept]
    d_attn = [k[1][4] for k in kept]
    part = width // groups
    aligned = part % 16 == 0 and groups == 2 * (inner_width // width)
    total_bits = groups.bit_length() - 1
    one_way = list(range(1, total_bits))
    other_way = one_way[::-1]
    if aligned:
        keep_o, send_o, keep_i, send_i = ffn_grads_split(
            my, d_outer_t, hidden, first_t, d_inner, groups
        )
        g_outer = sum_line(scatter_rest(keep_o, swap(send_o, "dp", 1), one_way))
        g_inner = scatter_rest(keep_i, swap(send_i, "dp", 1), other_way)
        g_inner = sum_line(g_inner.reshape(-1, width))
        g_outer = g_outer.T.astype(F32)
        g_inner = jnp.concatenate(jnp.split(g_inner, inner_width // width, axis=0), axis=1)
        g_inner = g_inner.astype(F32)
    else:
        g_outer = pair_product(d_outer_t, hidden)
        g_outer = g_outer.reshape(width, groups, -1).transpose(1, 2, 0)
        g_inner = pair_product(first_t, d_inner).reshape(groups, part, inner_width)
        g_outer = sum_line(scatter_bits(g_outer, [0] + one_way)).astype(F32)
        g_inner = scatter_bits(g_inner, [0] + other_way).reshape(-1, width)
        g_inner = sum_line(g_inner).reshape(part, inner_width).astype(F32)

    vec_two = jnp.zeros((8, width), F32)
    back = []
    returned = []
    for r in range(rows):
        q, k, v, e, inv, mix_t = kept[r][0][:6]
        d_res, d_mix_t = kept[r][1][5:7]
        outs = attn_back(
            cycle, q, k, v, e, inv, mix_t, d_mix_t, w_query, w_key, w_value, d_res, vec_two
        )
        returned.append(return_row(outs[:cycle]))
        vec_two = outs[-1]
        back.append(outs[cycle:-1])
    grad_in = spread(place, returned, F32)

    small = jnp.concatenate(
        [vec_two[:2], vec[:6], wide[0].reshape(-1, width), jnp.zeros((20, width), F32)], axis=0
    )
    x_t = [k[0][8] for k in kept]
    mix_t = [k[0][5] for k in kept]
    d_queries, d_keys, d_values = [[b[n] for b in back] for n in range(3)]
    if aligned:
        keep, send = attn_grads_split(
            my, x_t, d_queries, d_keys, d_values, mix_t, d_attn, small, groups
        )
        got = swap(send, "dp", 1)
        cut = (keep.shape[1] // 32) * 16
        late = jnp.concatenate(
            [
                scatter_rest(keep[:, :cut], got[:, :cut], one_way),
                scatter_rest(keep[:, cut:], got[:, cut:], other_way),
            ],
            axis=0,
        )
    else:
        late = [
            pair_product(x_t, d_queries),
            pair_product(x_t, d_keys),
            pair_product(x_t, d_values),
            pair_product(mix_t, d_attn),
        ]
        late = [value.reshape(groups, part, width) for value in late]
        late.append(jnp.broadcast_to(small.astype(BF16), (groups, 32, width)))
        late = scatter_bits(jnp.concatenate(late, axis=1), [0] + one_way)
    late = sum_line(late)
    if aligned:
        mats, vecs = late_results(late, groups, inner_width)
    else:
        mats = [late[w * part : (w + 1) * part].astype(F32) for w in range(4)]
        summed = late[4 * part :].astype(F32)
        vecs = [
            lax.dynamic_slice_in_dim(summed[n], my * part, part, 0) for n in range(8)
        ]
        count = inner_width // groups
        vecs.append(lax.dynamic_slice_in_dim(summed[8:12].reshape(-1), my * count, count, 0))
    g_query, g_key, g_value, g_attn = mats
    s_query, s_value, s_attn, s_gain, s_shift, s_outer, s_gain2, s_shift2, s_inner = vecs
    return (
        hidden_out,
        grad_in,
        g_query,
        s_query,
        g_key,
        g_value,
        s_value,
        g_attn,
        s_attn,
        s_gain,
        s_shift,
        g_inner,
        s_inner,
        g_outer,
        s_outer,
        s_gain2,
        s_shift2,
    )


def solution(mesh):
    placed = (P(None, "dp", "blk", None), P(None, "dp", None)) + (P(),) * 16
    placed = placed + (P(None, "dp", "blk", None),)
    return jax.shard_map(
        local,
        mesh=mesh,
        in_specs=placed,
        out_specs=(
            P(None, "dp", "blk", None),
            P(None, "dp", "blk", None),
            P("dp", None),
            P("dp"),
            P("dp", None),
            P("dp", None),
            P("dp"),
            P("dp", None),
            P("dp"),
            P("dp"),
            P("dp"),
            P("dp", None),
            P("dp"),
            P("dp", None),
            P("dp"),
            P("dp"),
            P("dp"),
        ),
        check_vma=False,
    )
```

```python
import functools

import jax
import jax.numpy as jnp
from jax import lax
from jax.experimental import pallas as pl
from jax.experimental.pallas import tpu as pltpu
from jax.sharding import PartitionSpec as P

HEADS = 12


EPS = 1e-12
F32 = jnp.float32
BF16 = jnp.bfloat16
NN = ((1,), (0,))
NT = ((1,), (1,))
LIMIT = 56 * 1024 * 1024
GROUP = 4
LANES = 128


def dot(left, right, dims=NN):
    return lax.dot_general(left, right, (dims, ((), ())), preferred_element_type=F32)


def params():
    return pltpu.CompilerParams(vmem_limit_bytes=LIMIT)


def cost():
    return pl.CostEstimate(flops=1000, bytes_accessed=1000, transcendentals=0)


def after(value, *others):
    return lax.optimization_barrier((value, others))[0]


def whole(shape):
    return pl.BlockSpec(shape, lambda *_: (0,) * len(shape))


def once(shape):
    return pl.BlockSpec(shape, lambda *_: (0,) * len(shape), pipeline_mode=pl.Buffered(1))


SMEM = pl.BlockSpec(memory_space=pltpu.SMEM)


def mask_kernel(blk_len, place_ref, len_ref, dam_ref, bits_ref, low_ref, high_ref):
    step = pl.program_id(0)
    chunk = dam_ref.shape[1]
    span = dam_ref.shape[2]
    rows = bits_ref.shape[0]
    low = dam_ref[0]
    for h in range(1, 8):
        low = low + (dam_ref[h] << h)
    high = dam_ref[8]
    for h in range(9, HEADS):
        high = high + (dam_ref[h] << (h - 8))
    at = pl.ds(pl.multiple_of(step * chunk, chunk), chunk)
    low_ref[at, :] = low.astype(F32).astype(BF16)
    high_ref[at, :] = high.astype(F32).astype(BF16)

    @pl.when(step == pl.num_programs(0) - 1)
    def _():
        place = place_ref[0]

        def places(axis):
            local = lax.broadcasted_iota(jnp.int32, (span, span), axis)
            return (((local // blk_len) ^ place) * blk_len) + local % blk_len

        for r in range(rows):
            first = len_ref[r, 0]
            second = first + len_ref[r, 1]

            def segment(at_place):
                one = jnp.where(at_place >= first, 1, 0)
                return one + jnp.where(at_place >= second, 1, 0)

            down = places(0)
            inside = (
                down
                - jnp.where(down >= first, first, 0)
                - jnp.where(down >= second, second - first, 0)
            )
            across = lax.broadcasted_iota(jnp.int32, (span, span), 1)
            pick = jnp.where(inside == across, 1.0, 0.0).astype(BF16)

            def moved(table):
                one = dot(pick, table, NT).astype(BF16)
                return dot(one, pick, NT).astype(jnp.int32)

            bits = moved(low_ref[...]) + (moved(high_ref[...]) << 8)
            bits_ref[r] = jnp.where(segment(down) == segment(places(1)), bits, 0)


def mask_bits(place, lengths, dam_mask, blk_len):
    heads, span, _ = dam_mask.shape
    rows = lengths.shape[0]
    chunk = 64
    return pl.pallas_call(
        functools.partial(mask_kernel, blk_len),
        grid=(span // chunk,),
        in_specs=[SMEM, SMEM, pl.BlockSpec((heads, chunk, span), lambda i: (0, i, 0))],
        out_specs=whole((rows, span, span)),
        out_shape=jax.ShapeDtypeStruct((rows, span, span), jnp.int32),
        scratch_shapes=[pltpu.VMEM((span, span), BF16)] * 2,
        compiler_params=params(),
        cost_estimate=cost(),
        name="mask_bits",
    )(place.reshape(1), lengths, dam_mask)


def attn_kernel(cycle, *refs):
    pieces = refs[:cycle]
    wq, wk, wv, bq, bv, bits_ref = refs[cycle : cycle + 6]
    q_out, k_out, v_out, e_out, inv_out, mix_t_out, mix_out, x_out, x_t_out, x_s = refs[cycle + 6 :]
    step = pl.program_id(0)
    blk_len = pieces[0].shape[0]
    span = x_s.shape[0]
    wide = wq.shape[1]

    @pl.when(step == 0)
    def _():
        for j in range(cycle):
            x_s[j * blk_len : (j + 1) * blk_len, :] = pieces[j][...]

    x = x_s[...]
    cols = pl.ds(pl.multiple_of(step * wide, wide), wide)
    x_cols = x_s[:, cols]
    x_out[...] = x_cols
    x_t_out[...] = x_cols.T
    q4 = ((dot(x, wq[...]) + bq[...].astype(F32)) * 0.125).astype(BF16)
    k4 = dot(x, wk[...])
    v4 = (dot(x, wv[...]) + bv[...].astype(F32)).astype(BF16)
    q_out[...] = q4
    k_out[...] = k4.astype(BF16)
    v_out[...] = v4
    v_t = v4.T
    lane = lax.broadcasted_iota(jnp.int32, (span, LANES), 1)
    ones = jnp.ones((16, span), BF16)
    half = span // 2
    for i in range(GROUP):
        pair, side = i // 2, i % 2
        k_pair = k4[:, pair * LANES : (pair + 1) * LANES]
        k_head = jnp.where((lane >= 64) == (side == 1), k_pair, 0.0).astype(BF16)
        bit = jnp.left_shift(jnp.int32(1), GROUP * step + i)
        for part in range(2):
            at = slice(part * half, (part + 1) * half)
            s = dot(k_head, q4[at, pair * LANES : (pair + 1) * LANES], NT)
            s = jnp.where((bits_ref[0, :, at] & bit) != 0, s, -1e30)
            top = jnp.max(s, axis=0, keepdims=True)
            e_out[i, :, at] = jnp.exp(s - top).astype(BF16)
        left = jnp.concatenate([v_t[64 * i : 64 * (i + 1), :], ones], axis=0)
        both = dot(left, e_out[i])
        inv = 1.0 / both[64:65, :]
        inv_out[0, i : i + 1, :] = inv
        mix_t_out[64 * i : 64 * (i + 1), :] = (both[:64, :] * inv).astype(BF16)
    mix_out[...] = mix_t_out[...].T


def attn_forward(pieces, w_query, w_key, w_value, b_query, b_value, bits, row):
    cycle = len(pieces)
    blk_len, width = pieces[0].shape
    span = blk_len * cycle
    wide = 64 * GROUP
    steps = width // wide
    col = pl.BlockSpec((span, wide), lambda g: (0, g))
    col_t = pl.BlockSpec((wide, span), lambda g: (g, 0))
    weight = pl.BlockSpec((width, wide), lambda g: (0, g))
    bias = pl.BlockSpec((1, wide), lambda g: (0, g))
    token = jax.ShapeDtypeStruct((span, width), BF16)
    token_t = jax.ShapeDtypeStruct((width, span), BF16)
    return pl.pallas_call(
        functools.partial(attn_kernel, cycle),
        grid=(steps,),
        in_specs=[once((blk_len, width))] * cycle
        + [weight] * 3
        + [bias] * 2
        + [pl.BlockSpec((1, span, span), lambda g: (row, 0, 0), pipeline_mode=pl.Buffered(1))],
        out_specs=[
            col,
            col,
            col,
            pl.BlockSpec((GROUP, span, span), lambda g: (g, 0, 0)),
            pl.BlockSpec((1, 8, span), lambda g: (g, 0, 0)),
            col_t,
            col,
            col,
            col_t,
        ],
        out_shape=[
            token,
            token,
            token,
            jax.ShapeDtypeStruct((HEADS, span, span), BF16),
            jax.ShapeDtypeStruct((steps, 8, span), F32),
            token_t,
            token,
            token,
            token_t,
        ],
        scratch_shapes=[pltpu.VMEM((span, width), BF16)],
        compiler_params=params(),
        cost_estimate=cost(),
        name="attn_forward",
    )(*pieces, w_query, w_key, w_value, b_query, b_value, bits)


def norm_forward(values):
    centred = values - jnp.mean(values, axis=-1, keepdims=True)
    inv_scale = lax.rsqrt(jnp.mean(centred * centred, axis=-1, keepdims=True) + EPS)
    return (centred * inv_scale, inv_scale)


def norm_back(grad_normed, normed, inv_scale):
    mean_grad = jnp.mean(grad_normed, axis=-1, keepdims=True)
    mean_cross = jnp.mean(grad_normed * normed, axis=-1, keepdims=True)
    return inv_scale * (grad_normed - mean_grad - normed * mean_cross)


def gelu_parts(values):
    cdf = 0.5 + 0.5 * lax.erf(values * 0.7071067811865476)
    slope = cdf + values * (jnp.exp(-0.5 * values * values) * 0.3989422804014327)
    return values * cdf, slope


def total(values):
    return jnp.sum(values, axis=0, keepdims=True)


def ffn_kernel(cycle, *refs):
    place_ref, g_ref = refs[:2]
    refs = refs[2:]
    (x_ref, mix_ref, w_o, w_in, w_out, b_o, gain1, shift1, b_in, b_out, gain2, shift2) = refs[:12]
    (vec_in, wide_in) = refs[12:14]
    outs = refs[14:]
    h_out = outs[:cycle]
    (
        first_t_out,
        hidden_out,
        d_inner_out,
        d_outer_t_out,
        d_attn_out,
        d_res_out,
        d_mix_t_out,
        vec_out,
        wide_out,
        wo_s,
        win_s,
        wout_s,
        slope_s,
        g_s,
        sems,
    ) = outs[cycle:]
    copies = [
        pltpu.make_async_copy(src, dst, sems.at[i])
        for i, (src, dst) in enumerate(((w_o, wo_s), (w_in, win_s), (w_out, wout_s)))
    ]
    for copy in copies:
        copy.start()
    blk_len, width = g_ref.shape[2:]
    inner_width = win_s.shape[1]
    for j in range(cycle):
        g_s[j * blk_len : (j + 1) * blk_len, :] = g_ref[place_ref[0] ^ j, 0]
    copies[0].wait()
    residual = x_ref[...].astype(F32) + dot(mix_ref[...], wo_s[...]) + b_o[...].astype(F32)
    normed_one, scale_one = norm_forward(residual)
    first = normed_one * gain1[...].astype(F32) + shift1[...].astype(F32)
    first_low = first.astype(BF16)
    first_t_out[...] = first_low.T
    copies[1].wait()
    chunks = [slice(i * width, (i + 1) * width) for i in range(inner_width // width)]
    for at in chunks:
        inner = dot(first_low, win_s[:, at]) + b_in[:, at].astype(F32)
        hidden, slope = gelu_parts(inner)
        hidden_out[:, at] = hidden.astype(BF16)
        slope_s[:, at] = slope.astype(BF16)
    copies[2].wait()
    second = first + dot(hidden_out[...], wout_s[...]) + b_out[...].astype(F32)
    normed_two, scale_two = norm_forward(second)
    result = (normed_two * gain2[...].astype(F32) + shift2[...].astype(F32)).astype(BF16)
    for j in range(cycle):
        h_out[j][...] = result[j * blk_len : (j + 1) * blk_len, :]
    grad = g_s[...].astype(F32)
    vec_out[4:5, :] = vec_in[4:5, :] + total(grad * normed_two)
    vec_out[5:6, :] = vec_in[5:6, :] + total(grad)
    d_second = norm_back(grad * gain2[...].astype(F32), normed_two, scale_two)
    d_outer = d_second.astype(BF16)
    d_outer_t_out[...] = d_outer.T
    vec_out[3:4, :] = vec_in[3:4, :] + total(d_outer.astype(F32))
    for at in chunks:
        d_hidden = dot(d_outer, wout_s[at, :], NT)
        d_inner = (d_hidden * slope_s[:, at].astype(F32)).astype(BF16)
        d_inner_out[:, at] = d_inner
        wide_out[0:1, at] = wide_in[0:1, at] + total(d_inner.astype(F32))
    d_first = d_second + dot(d_inner_out[...], win_s[...], NT)
    vec_out[1:2, :] = vec_in[1:2, :] + total(d_first * normed_one)
    vec_out[2:3, :] = vec_in[2:3, :] + total(d_first)
    d_res = norm_back(d_first * gain1[...].astype(F32), normed_one, scale_one)
    d_res_out[...] = d_res
    d_attn = d_res.astype(BF16)
    d_attn_out[...] = d_attn
    vec_out[0:1, :] = vec_in[0:1, :] + total(d_attn.astype(F32))
    d_mix_t_out[...] = dot(wo_s[...], d_attn, NT).astype(BF16)


def ffn_both(place, grads, row, x, mixed, weights, vectors, vec_in, wide_in):
    cycle, _, blk_len, _ = grads.shape
    span, width = x.shape
    inner_width = weights[1].shape[1]
    token = jax.ShapeDtypeStruct((span, width), BF16)
    token_t = jax.ShapeDtypeStruct((width, span), BF16)
    wide = jax.ShapeDtypeStruct((span, inner_width), BF16)
    out_shape = [jax.ShapeDtypeStruct((blk_len, width), BF16)] * cycle + [
        token_t,
        wide,
        wide,
        token_t,
        token,
        jax.ShapeDtypeStruct((span, width), F32),
        token_t,
        jax.ShapeDtypeStruct((8, width), F32),
        jax.ShapeDtypeStruct((8, inner_width), F32),
    ]
    vmem = pl.BlockSpec(memory_space=pltpu.VMEM)
    return pl.pallas_call(
        functools.partial(ffn_kernel, cycle),
        grid=(1,),
        in_specs=[SMEM, pl.BlockSpec((cycle, 1, blk_len, width), lambda i: (0, row, 0, 0))]
        + [vmem] * 2
        + [pl.BlockSpec(memory_space=pl.ANY)] * 3
        + [vmem] * (len(vectors) + 2),
        out_specs=[vmem] * len(out_shape),
        out_shape=out_shape,
        scratch_shapes=[
            pltpu.VMEM(weights[0].shape, BF16),
            pltpu.VMEM(weights[1].shape, BF16),
            pltpu.VMEM(weights[2].shape, BF16),
            pltpu.VMEM((span, inner_width), BF16),
            pltpu.VMEM((span, width), BF16),
            pltpu.SemaphoreType.DMA((3,)),
        ],
        compiler_params=params(),
        cost_estimate=cost(),
        name="ffn_both",
    )(place.reshape(1), grads, x, mixed, *weights, *vectors, vec_in, wide_in)


def place_parts(tile_ref, my, keep_ref, send_ref, part, put):
    groups = tile_ref.shape[0] // part
    for p in range(groups):
        at = pl.ds(pl.multiple_of((my ^ p) * part, 16), part)
        put(send_ref if p % 2 else keep_ref, p // 2, tile_ref[at, :])


def outer_grad_kernel(dot0, dot1, hid0, hid1, out):
    outer = (dot(dot0[...], hid0[...]) + dot(dot1[...], hid1[...])).astype(BF16)
    half = outer.shape[1] // 2
    out[0] = outer[:, :half]
    out[1] = outer[:, half:]


def outer_grads(d_outer_t, hidden):
    width, span = d_outer_t[0].shape
    steps = hidden[0].shape[1] // width
    half = width // 2
    lhs = pl.BlockSpec((width, span), lambda i: (0, 0), pipeline_mode=pl.Buffered(1))
    rhs = pl.BlockSpec((span, width), lambda i: (0, i))
    return pl.pallas_call(
        outer_grad_kernel,
        grid=(steps,),
        in_specs=[lhs, lhs, rhs, rhs],
        out_specs=pl.BlockSpec((2, width, half), lambda i: (i, 0, 0)),
        out_shape=jax.ShapeDtypeStruct((2 * steps, width, half), BF16),
        compiler_params=params(),
        cost_estimate=cost(),
        name="outer_grads",
    )(*d_outer_t, *hidden)


def inner_grad_kernel(my_ref, ft0, ft1, din0, din1, mt0, mt1, da0, da1, keep, send, tile_s):
    last = pl.program_id(0) == pl.num_programs(0) - 1

    @pl.when(jnp.logical_not(last))
    def _():
        tile_s[...] = (dot(ft0[...], din0[...]) + dot(ft1[...], din1[...])).astype(BF16)

    @pl.when(last)
    def _():
        tile_s[...] = (dot(mt0[...], da0[...]) + dot(mt1[...], da1[...])).astype(BF16)

    def put(ref, at, value):
        ref[at, 0] = value

    place_parts(tile_s, my_ref[0], keep, send, keep.shape[2], put)


def inner_grads(my, first_t, d_inner, mix_t, d_attn, groups):
    width, span = first_t[0].shape
    steps = d_inner[0].shape[1] // width
    part = width // groups
    lhs = pl.BlockSpec((width, span), lambda i: (0, 0), pipeline_mode=pl.Buffered(1))
    rhs = pl.BlockSpec((span, width), lambda i: (0, jnp.minimum(i, steps - 1)))
    one = pl.BlockSpec((span, width), lambda i: (0, 0), pipeline_mode=pl.Buffered(1))
    shape = jax.ShapeDtypeStruct((groups // 2, steps + 1, part, width), BF16)
    return pl.pallas_call(
        inner_grad_kernel,
        grid=(steps + 1,),
        in_specs=[SMEM, lhs, lhs, rhs, rhs, lhs, lhs, one, one],
        out_specs=[pl.BlockSpec((groups // 2, 1, part, width), lambda i: (0, i, 0, 0))] * 2,
        out_shape=[shape, shape],
        scratch_shapes=[pltpu.VMEM((width, width), BF16)],
        compiler_params=params(),
        cost_estimate=cost(),
        name="inner_grads",
    )(my.reshape(1), *first_t, *d_inner, *mix_t, *d_attn)


def pair_product_kernel(a0, a1, b0, b1, out):
    out[...] = (dot(a0[...], b0[...]) + dot(a1[...], b1[...])).astype(BF16)


def pair_product(left, right):
    depth = left[0].shape[1]
    rows = left[0].shape[0]
    columns = right[0].shape[1]
    wide = 768
    lhs = pl.BlockSpec((rows, depth), lambda i: (0, 0))
    rhs = pl.BlockSpec((depth, wide), lambda i: (0, i))
    return pl.pallas_call(
        pair_product_kernel,
        grid=(columns // wide,),
        in_specs=[lhs, lhs, rhs, rhs],
        out_specs=pl.BlockSpec((rows, wide), lambda i: (0, i)),
        out_shape=jax.ShapeDtypeStruct((rows, columns), BF16),
        compiler_params=params(),
        cost_estimate=cost(),
        name="pair_product",
    )(*left, *right)


def attn_back_kernel(cycle, *refs):
    (q_ref, k_ref, v_ref, e_ref, inv_ref, mix_t, d_mix_t, wq, wk, wv, d_res, vec_in) = refs[:12]
    g_out = refs[12 : 12 + cycle]
    dq_out, dk_out, dv_out, vec_out, acc, dq_t = refs[12 + cycle :]
    step = pl.program_id(0)
    span = q_ref.shape[0]
    blk_len = span // cycle
    k_t = k_ref[...].T
    lane = lax.broadcasted_iota(jnp.int32, (span, LANES), 1)
    blank = jnp.zeros((64, span), BF16)
    for pair in range(GROUP // 2):
        at = slice(pair * LANES, (pair + 1) * LANES)
        q_pair = q_ref[:, at]
        v_pair = v_ref[:, at]
        d_keys = []
        d_values = None
        for side in range(2):
            i = 2 * pair + side
            mine = slice(64 * i, 64 * (i + 1))
            scaled = d_mix_t[mine, :].astype(F32) * inv_ref[0, i : i + 1, :]
            cross = jnp.sum(scaled * mix_t[mine, :].astype(F32), axis=0, keepdims=True)
            scaled = scaled.astype(BF16)
            padded = jnp.concatenate([blank, scaled] if side else [scaled, blank], axis=0)
            d_probs = dot(v_pair, padded)
            d_scores = (e_ref[i].astype(F32) * (d_probs - cross)).astype(BF16)
            d_keys.append(dot(d_scores, q_pair))
            d_value = dot(e_ref[i], padded, NT)
            d_values = d_value if d_values is None else d_values + d_value
            dq_t[mine, :] = dot(k_t[mine, :], d_scores)
        dk_out[:, at] = jnp.where(lane >= 64, d_keys[1], d_keys[0]).astype(BF16)
        dv_out[:, at] = d_values.astype(BF16)
    dq_out[...] = (dq_t[...] * 0.125).T.astype(BF16)
    vec_out[...] = vec_in[...]
    vec_out[0:1, :] += total(dq_out[...].astype(F32))
    vec_out[1:2, :] += total(dv_out[...].astype(F32))
    more = dot(dq_out[...], wq[...], NT) + dot(dk_out[...], wk[...], NT)
    more = more + dot(dv_out[...], wv[...], NT)

    @pl.when(step == 0)
    def _():
        acc[...] = d_res[...] + more

    @pl.when(step > 0)
    def _():
        acc[...] += more

    @pl.when(step == pl.num_programs(0) - 1)
    def _():
        for j in range(cycle):
            g_out[j][...] = acc[j * blk_len : (j + 1) * blk_len, :].astype(BF16)


def attn_back(cycle, q, k, v, e, inv, mix_t, d_mix_t, w_query, w_key, w_value, d_res, vec_in):
    span, width = q.shape
    blk_len = span // cycle
    wide = 64 * GROUP
    steps = width // wide
    col = pl.BlockSpec((span, wide), lambda g: (0, g))
    col_t = pl.BlockSpec((wide, span), lambda g: (g, 0))
    weight = pl.BlockSpec((width, wide), lambda g: (0, g))
    small = pl.BlockSpec((8, wide), lambda g: (0, g))
    token = jax.ShapeDtypeStruct((span, width), BF16)
    return pl.pallas_call(
        functools.partial(attn_back_kernel, cycle),
        grid=(steps,),
        in_specs=[
            col,
            col,
            col,
            pl.BlockSpec((GROUP, span, span), lambda g: (g, 0, 0)),
            pl.BlockSpec((1, 8, span), lambda g: (g, 0, 0)),
            col_t,
            col_t,
            weight,
            weight,
            weight,
            once((span, width)),
            small,
        ],
        out_specs=[whole((blk_len, width))] * cycle + [col] * 3 + [small],
        out_shape=[jax.ShapeDtypeStruct((blk_len, width), BF16)] * cycle
        + [token] * 3
        + [jax.ShapeDtypeStruct((8, width), F32)],
        scratch_shapes=[pltpu.VMEM((span, width), F32), pltpu.VMEM((wide, span), F32)],
        compiler_params=params(),
        cost_estimate=cost(),
        name="attn_back",
    )(q, k, v, e, inv, mix_t, d_mix_t, w_query, w_key, w_value, d_res, vec_in)


def attn_grad_kernel(my_ref, xt0, xt1, dq0, dq1, dk0, dk1, dv0, dv1, vec, keep, send, tile_s):
    my = my_ref[0]
    part = tile_s.shape[0] // (2 * keep.shape[0])
    work = (
        (xt0, dq0, xt1, dq1),
        (xt0, dk0, xt1, dk1),
        (xt0, dv0, xt1, dv1),
    )
    for w, (a0, b0, a1, b1) in enumerate(work):
        tile_s[...] = (dot(a0[...], b0[...]) + dot(a1[...], b1[...])).astype(BF16)

        def put(ref, at, value):
            ref[at, w * part : (w + 1) * part, :] = value

        place_parts(tile_s, my, keep, send, part, put)
    low = vec[...].astype(BF16)
    for p in range(keep.shape[0]):
        keep[p, 3 * part :, :] = low
        send[p, 3 * part :, :] = low


def attn_grads_split(my, x_t, d_queries, d_keys, d_values, vec, groups):
    width, span = x_t[0].shape
    part = width // groups
    vmem = pl.BlockSpec(memory_space=pltpu.VMEM)
    shape = jax.ShapeDtypeStruct((groups // 2, 3 * part + 32, width), BF16)
    return pl.pallas_call(
        attn_grad_kernel,
        in_specs=[SMEM] + [vmem] * 9,
        out_specs=[vmem] * 2,
        out_shape=[shape] * 2,
        scratch_shapes=[pltpu.VMEM((width, width), BF16)],
        compiler_params=params(),
        cost_estimate=cost(),
        name="attn_grads",
    )(my.reshape(1), *x_t, *d_queries, *d_keys, *d_values, vec)


def swap(values, axis, mask):
    size = lax.axis_size(axis)
    return lax.ppermute(values, axis, [(i, i ^ mask) for i in range(size)])


def added(left, right):
    return (left.astype(F32) + right.astype(F32)).astype(BF16)


def scatter_rest(held, bits):
    for at, bit in enumerate(bits):
        rest = bits[at + 1 :]
        size = held.shape[0]
        alive = [0]
        for other in sorted([bit] + rest):
            alive = alive + [p | (1 << (other - 1)) for p in alive]
        keep_at = [n for n, p in enumerate(alive) if not (p >> (bit - 1)) & 1]
        send_at = [n for n, p in enumerate(alive) if (p >> (bit - 1)) & 1]
        assert size == len(alive)
        send = jnp.stack([held[n] for n in send_at])
        keep = jnp.stack([held[n] for n in keep_at])
        got = swap(send, "dp", 1 << bit)
        held = added(keep, got)
    return held[0]


def scatter_bits(blocks, order):
    size = lax.axis_size("dp")
    bits = size.bit_length() - 1
    place = lax.axis_index("dp")
    held = blocks.reshape((2,) * bits + blocks.shape[1:])
    left = list(range(bits - 1, -1, -1))
    for bit in order:
        axis = left.index(bit)
        mine = (place >> bit) & 1
        keep = lax.dynamic_index_in_dim(held, mine, axis, keepdims=False)
        send = lax.dynamic_index_in_dim(held, 1 - mine, axis, keepdims=False)
        held = added(keep, swap(send, "dp", 1 << bit))
        left.remove(bit)
    return held


def line_scatter(rows):
    size = lax.axis_size("blk")
    place = lax.axis_index("blk")
    share = rows.shape[0] // size
    blocks = rows.reshape((size, share) + rows.shape[1:])
    parts = [lax.dynamic_index_in_dim(blocks, place ^ j, 0, keepdims=False) for j in range(size)]
    held = parts[0].astype(F32)
    for part in [swap(parts[j], "blk", j) for j in range(1, size)]:
        held = held + part.astype(F32)
    return held.astype(BF16)


def line_gather(share):
    return [share] + [swap(share, "blk", j) for j in range(1, lax.axis_size("blk"))]


def line_join(parts):
    place = lax.axis_index("blk")
    return jnp.take(jnp.stack(parts), jnp.arange(len(parts)) ^ place, axis=0).reshape(
        (-1,) + parts[0].shape[1:]
    )


def join(place, parts, whole_ref):
    share = parts[0].shape[0]
    for j, piece in enumerate(parts):
        at = pl.ds(pl.multiple_of((place ^ j) * share, 8), share)
        whole_ref[at, :] = piece[...].astype(F32)


def early_kernel(cycle, place_ref, *refs):
    outer, inner = refs[:cycle], refs[cycle : 2 * cycle]
    outer_out, inner_out, attn_out, outer_s, inner_s = refs[2 * cycle :]
    place = place_ref[0]
    join(place, outer, outer_s)
    outer_out[...] = outer_s[...].T
    join(place, inner, inner_s)
    part, wide = inner_out.shape
    width = inner_s.shape[1]
    count = wide // width
    for i in range(count):
        inner_out[:, i * width : (i + 1) * width] = inner_s[i * part : (i + 1) * part, :]
    attn_out[...] = inner_s[count * part :, :]


def early_results(place, outer, inner, part):
    cycle = len(outer)
    rows, half = cycle * outer[0].shape[0], outer[0].shape[1]
    tall, width = cycle * inner[0].shape[0], inner[0].shape[1]
    vmem = pl.BlockSpec(memory_space=pltpu.VMEM)
    return pl.pallas_call(
        functools.partial(early_kernel, cycle),
        in_specs=[SMEM] + [vmem] * (2 * cycle),
        out_specs=[vmem] * 3,
        out_shape=[
            jax.ShapeDtypeStruct((half, rows), F32),
            jax.ShapeDtypeStruct((part, (tall // part - 1) * width), F32),
            jax.ShapeDtypeStruct((part, width), F32),
        ],
        scratch_shapes=[pltpu.VMEM((rows, half), F32), pltpu.VMEM((tall, width), F32)],
        compiler_params=params(),
        cost_estimate=cost(),
        name="early_results",
    )(place.reshape(1), *outer, *inner)


def late_kernel(cycle, lanes_ref, *refs):
    late = refs[-1]
    join(lanes_ref[3], refs[:cycle], late)
    outs = refs[cycle:-1]
    part = outs[0].shape[0]
    for w in range(3):
        outs[w][...] = late[w * part : (w + 1) * part, :]
    vec = late[3 * part :, :].astype(BF16)
    width = vec.shape[1]
    size = outs[3].shape[1]

    def picked(start, count):
        lanes = -(-count // LANES) * LANES
        source = lax.broadcasted_iota(jnp.int32, (width, lanes), 0)
        target = lax.broadcasted_iota(jnp.int32, (width, lanes), 1)
        return jnp.where(source == target + start, 1.0, 0.0).astype(BF16)

    narrow = dot(vec, picked(lanes_ref[0], size))
    for n in range(8):
        outs[3 + n][...] = narrow[n : n + 1, :size]
    count = outs[11].shape[1]
    broad = dot(vec, picked(lanes_ref[1], count))
    row = lax.broadcasted_iota(jnp.int32, broad.shape, 0)
    broad = jnp.where(row == lanes_ref[2], broad, 0.0)
    outs[11][...] = total(broad)[:, :count]


def late_results(place, parts, groups, inner_width):
    cycle = len(parts)
    width = parts[0].shape[1]
    rows = cycle * parts[0].shape[0]
    part = (rows - 32) // 3
    size = width // groups
    count = inner_width // groups
    my = lax.axis_index("dp")
    start = my * count
    lanes = jnp.stack([my * size, start % width, 8 + start // width, place]).astype(jnp.int32)
    vmem = pl.BlockSpec(memory_space=pltpu.VMEM)
    shapes = (
        [jax.ShapeDtypeStruct((part, width), F32)] * 3
        + [jax.ShapeDtypeStruct((1, size), F32)] * 8
        + [jax.ShapeDtypeStruct((1, count), F32)]
    )
    outs = pl.pallas_call(
        functools.partial(late_kernel, cycle),
        in_specs=[SMEM] + [vmem] * cycle,
        out_specs=[vmem] * len(shapes),
        out_shape=shapes,
        scratch_shapes=[pltpu.VMEM((rows, width), F32)],
        compiler_params=params(),
        cost_estimate=cost(),
        name="late_results",
    )(lanes, *parts)
    return list(outs[:3]), [value.reshape(-1) for value in outs[3:]]


def spread_kernel(cycle, rows, place_ref, *refs):
    pieces = refs[:-1]
    out = refs[-1]
    for r in range(rows):
        for j in range(cycle):
            out[place_ref[0] ^ j, r] = pieces[r * cycle + j][...].astype(out.dtype)


def spread(place, pieces, dtype):
    rows, cycle = len(pieces), len(pieces[0])
    blk_len, width = pieces[0][0].shape
    vmem = pl.BlockSpec(memory_space=pltpu.VMEM)
    return pl.pallas_call(
        functools.partial(spread_kernel, cycle, rows),
        in_specs=[SMEM] + [vmem] * (rows * cycle),
        out_specs=vmem,
        out_shape=jax.ShapeDtypeStruct((cycle, rows, blk_len, width), dtype),
        compiler_params=params(),
        cost_estimate=cost(),
        name="spread",
    )(place.reshape(1), *[piece for row in pieces for piece in row])


def local(
    hidden_in,
    seq_lengths,
    dam_mask,
    w_query,
    b_query,
    w_key,
    w_value,
    b_value,
    w_attn_out,
    b_attn_out,
    gain_attn,
    shift_attn,
    w_inner,
    b_inner,
    w_outer,
    b_outer,
    gain_ffn,
    shift_ffn,
    grad_out,
):
    micro, rows, blk_len, width = hidden_in.shape
    cycle = lax.axis_size("blk")
    groups = lax.axis_size("dp")
    inner_width = w_inner.shape[1]
    place = lax.axis_index("blk")
    my = lax.axis_index("dp")

    def gather_row(values, row):
        mine = values[:, row]
        parts = [lax.dynamic_index_in_dim(mine, place ^ j, 0, keepdims=False) for j in range(cycle)]
        return [parts[0]] + [swap(parts[j], "blk", j) for j in range(1, cycle)]

    def return_row(parts):
        return [parts[0]] + [swap(parts[j], "blk", j) for j in range(1, cycle)]

    def flat(vector):
        return vector.reshape(1, -1)

    tokens = [gather_row(hidden_in, 0)]
    lengths = lax.dynamic_index_in_dim(seq_lengths, place, 0, keepdims=False)
    bits = mask_bits(place, lengths, dam_mask, blk_len)
    tokens += [gather_row(after(hidden_in, bits), r) for r in range(1, rows)]
    vectors = [
        flat(v)
        for v in (b_attn_out, gain_attn, shift_attn, b_inner, b_outer, gain_ffn, shift_ffn)
    ]
    ahead = []
    for r in range(rows):
        pieces = tokens[r]
        if r:
            pieces = [after(pieces[0], ahead[-1][0])] + pieces[1:]
        ahead.append(
            attn_forward(pieces, w_query, w_key, w_value, flat(b_query), flat(b_value), bits, r)
        )
    grads = lax.all_to_all(after(grad_out, ahead[0][0]), "blk", 0, 0, tiled=True)
    vec = jnp.zeros((8, width), F32)
    wide = jnp.zeros((8, inner_width), F32)
    kept = []
    results = []
    for r in range(rows):
        x, mixed = ahead[r][7], ahead[r][6]
        if r == 0:
            x = after(x, ahead[-1][0])
        result = ffn_both(
            place, grads, r, x, mixed, (w_attn_out, w_inner, w_outer), vectors, vec, wide
        )
        results.append(return_row(result[:cycle]))
        vec, wide = result[-2:]
        kept.append((ahead[r], result[cycle:-2]))
    hidden_out = spread(place, results, BF16)

    first_t = [k[1][0] for k in kept]
    hidden = [k[1][1] for k in kept]
    d_inner = [k[1][2] for k in kept]
    d_outer_t = [k[1][3] for k in kept]
    d_attn = [k[1][4] for k in kept]
    part = width // groups
    aligned = part % 16 == 0 and groups == 2 * (inner_width // width)
    total_bits = groups.bit_length() - 1
    one_way = list(range(1, total_bits))
    other_way = one_way[::-1]
    if aligned:
        outer = outer_grads(d_outer_t, hidden)
        d_inner = [after(d_inner[0], outer)] + d_inner[1:]
        mix_t = [k[0][5] for k in kept]
        inner_keep, inner_send = inner_grads(my, first_t, d_inner, mix_t, d_attn, groups)
        outer = lax.psum_scatter(outer, "dp", scatter_dimension=0, tiled=False)
        ready = inner_keep
    else:
        outer = pair_product(d_outer_t, hidden)
        outer = outer.reshape(width, groups, -1).transpose(1, 2, 0)
        outer = lax.psum_scatter(outer, "dp", scatter_dimension=0, tiled=False)
        inner = pair_product(first_t, d_inner).reshape(groups, part, inner_width)
        attn = pair_product([k[0][5] for k in kept], d_attn).reshape(groups, part, width)
        pieces = jnp.split(inner, inner_width // width, axis=2) + [attn]
        inner = scatter_bits(jnp.concatenate(pieces, axis=1), [0] + other_way)
        ready = inner

    vec_two = jnp.zeros((8, width), F32)
    back = []
    returned = []
    for r in range(rows):
        q, k, v, e, inv, mix_t = kept[r][0][:6]
        d_res, d_mix_t = kept[r][1][5:7]
        d_res = after(d_res, ready)
        outs = attn_back(
            cycle, q, k, v, e, inv, mix_t, d_mix_t, w_query, w_key, w_value, d_res, vec_two
        )
        returned.append(return_row(outs[:cycle]))
        vec_two = outs[-1]
        back.append(outs[cycle:-1])
        if aligned and r == 0:
            inner = added(inner_keep, swap(inner_send, "dp", 1))
            ready = (inner, hidden_out)
    if aligned:
        inner = scatter_rest(inner, other_way).reshape(-1, width)
    grad_in = spread(place, returned, F32)

    small = jnp.concatenate(
        [vec_two[:2], vec[:6], wide[0].reshape(-1, width), jnp.zeros((20, width), F32)], axis=0
    )
    x_t = [k[0][8] for k in kept]
    d_queries, d_keys, d_values = [[b[n] for b in back] for n in range(3)]
    if aligned:
        keep, send = attn_grads_split(
            my, x_t, d_queries, d_keys, d_values, small, groups
        )
        held = added(keep, swap(send, "dp", 1))
        cut = (keep.shape[1] // 32) * 16
        late = jnp.concatenate(
            [scatter_rest(held[:, :cut], one_way), scatter_rest(held[:, cut:], other_way)], axis=0
        )
    else:
        late = [
            pair_product(x_t, d_queries),
            pair_product(x_t, d_keys),
            pair_product(x_t, d_values),
        ]
        late = [value.reshape(groups, part, width) for value in late]
        late.append(jnp.broadcast_to(small.astype(BF16), (groups, 32, width)))
        late = scatter_bits(jnp.concatenate(late, axis=1), [0] + one_way)
    outer = line_gather(line_scatter(after(outer, d_queries)))
    inner = line_gather(line_scatter(inner))
    late = line_gather(line_scatter(late))
    if aligned:
        g_outer, g_inner, g_attn = early_results(place, outer, inner, part)
        mats, vecs = late_results(place, late, groups, inner_width)
    else:
        g_outer = line_join(outer).astype(F32)
        inner = line_join(inner).astype(F32)
        g_inner = jnp.concatenate(
            [inner[i * part : (i + 1) * part] for i in range(inner_width // width)], axis=1
        )
        g_attn = inner[part * (inner_width // width) :]
        late = line_join(late)
        mats = [late[w * part : (w + 1) * part].astype(F32) for w in range(3)]
        summed = late[3 * part :].astype(F32)
        vecs = [
            lax.dynamic_slice_in_dim(summed[n], my * part, part, 0) for n in range(8)
        ]
        count = inner_width // groups
        vecs.append(lax.dynamic_slice_in_dim(summed[8:12].reshape(-1), my * count, count, 0))
    g_query, g_key, g_value = mats
    s_query, s_value, s_attn, s_gain, s_shift, s_outer, s_gain2, s_shift2, s_inner = vecs
    return (
        hidden_out,
        grad_in,
        g_query,
        s_query,
        g_key,
        g_value,
        s_value,
        g_attn,
        s_attn,
        s_gain,
        s_shift,
        g_inner,
        s_inner,
        g_outer,
        s_outer,
        s_gain2,
        s_shift2,
    )


def solution(mesh):
    placed = (P(None, "dp", "blk", None), P(None, "dp", None)) + (P(),) * 16
    placed = placed + (P(None, "dp", "blk", None),)
    return jax.shard_map(
        local,
        mesh=mesh,
        in_specs=placed,
        out_specs=(
            P(None, "dp", "blk", None),
            P(None, "dp", "blk", None),
            P("dp", None),
            P("dp"),
            P("dp", None),
            P("dp", None),
            P("dp"),
            P("dp", None),
            P("dp"),
            P("dp"),
            P("dp"),
            P("dp", None),
            P("dp"),
            P("dp", None),
            P("dp"),
            P("dp"),
            P("dp"),
        ),
        check_vma=False,
    )
```

```python
import functools

import jax
import jax.numpy as jnp
from jax import lax
from jax.experimental import pallas as pl
from jax.experimental.pallas import tpu as pltpu
from jax.sharding import PartitionSpec as P

HEADS = 12


EPS = 1e-12
F32 = jnp.float32
BF16 = jnp.bfloat16
NN = ((1,), (0,))
NT = ((1,), (1,))
LIMIT = 56 * 1024 * 1024
GROUP = 4
LANES = 128


def dot(left, right, dims=NN):
    return lax.dot_general(left, right, (dims, ((), ())), preferred_element_type=F32)


def params():
    return pltpu.CompilerParams(vmem_limit_bytes=LIMIT)


SCALE = 1.0


def cost(flops=1e9):
    return pl.CostEstimate(flops=int(SCALE * flops), bytes_accessed=1000, transcendentals=0)


def after(value, *others):
    return lax.optimization_barrier((value, others))[0]


def whole(shape):
    return pl.BlockSpec(shape, lambda *_: (0,) * len(shape))


def once(shape):
    return pl.BlockSpec(shape, lambda *_: (0,) * len(shape), pipeline_mode=pl.Buffered(1))


SMEM = pl.BlockSpec(memory_space=pltpu.SMEM)


def mask_kernel(len_ref, dam_ref, bits_ref, low_ref, high_ref):
    step = pl.program_id(0)
    chunk = dam_ref.shape[1]
    span = dam_ref.shape[2]
    rows = bits_ref.shape[0]
    low = dam_ref[0]
    for h in range(1, 8):
        low = low + (dam_ref[h] << h)
    high = dam_ref[8]
    for h in range(9, HEADS):
        high = high + (dam_ref[h] << (h - 8))
    at = pl.ds(pl.multiple_of(step * chunk, chunk), chunk)
    low_ref[at, :] = low.astype(F32).astype(BF16)
    high_ref[at, :] = high.astype(F32).astype(BF16)

    @pl.when(step == pl.num_programs(0) - 1)
    def _():
        def places(axis):
            return lax.broadcasted_iota(jnp.int32, (span, span), axis)

        for r in range(rows):
            first = len_ref[r, 0]
            second = first + len_ref[r, 1]

            def segment(at_place):
                one = jnp.where(at_place >= first, 1, 0)
                return one + jnp.where(at_place >= second, 1, 0)

            down = places(0)
            inside = (
                down
                - jnp.where(down >= first, first, 0)
                - jnp.where(down >= second, second - first, 0)
            )
            across = lax.broadcasted_iota(jnp.int32, (span, span), 1)
            pick = jnp.where(inside == across, 1.0, 0.0).astype(BF16)

            def moved(table):
                one = dot(pick, table, NT).astype(BF16)
                return dot(one, pick, NT).astype(jnp.int32)

            bits = moved(low_ref[...]) + (moved(high_ref[...]) << 8)
            bits_ref[r] = jnp.where(segment(down) == segment(places(1)), bits, 0)


def mask_bits(lengths, dam_mask):
    heads, span, _ = dam_mask.shape
    rows = lengths.shape[0]
    chunk = 64
    return pl.pallas_call(
        mask_kernel,
        grid=(span // chunk,),
        in_specs=[SMEM, pl.BlockSpec((heads, chunk, span), lambda i: (0, i, 0))],
        out_specs=whole((rows, span, span)),
        out_shape=jax.ShapeDtypeStruct((rows, span, span), jnp.int32),
        scratch_shapes=[pltpu.VMEM((span, span), BF16)] * 2,
        compiler_params=params(),
        cost_estimate=cost(12e9),
        name="mask_bits",
    )(lengths, dam_mask)


def attn_kernel(
    x_ref, wq, wk, wv, bq, bv, bits_ref, q_out, k_out, v_out, e_out, inv_out, mix_t_out, mix_out, x_t_out
):
    step = pl.program_id(0)
    span = x_ref.shape[0]
    wide = wq.shape[1]
    x = x_ref[...]
    cols = pl.ds(pl.multiple_of(step * wide, wide), wide)
    x_t_out[...] = x_ref[:, cols].T
    q4 = ((dot(x, wq[...]) + bq[...].astype(F32)) * 0.125).astype(BF16)
    k4 = dot(x, wk[...])
    v4 = (dot(x, wv[...]) + bv[...].astype(F32)).astype(BF16)
    q_out[...] = q4
    k_out[...] = k4.astype(BF16)
    v_out[...] = v4
    v_t = v4.T
    lane = lax.broadcasted_iota(jnp.int32, (span, LANES), 1)
    ones = jnp.ones((16, span), BF16)
    half = span // 2
    for i in range(GROUP):
        pair, side = i // 2, i % 2
        k_pair = k4[:, pair * LANES : (pair + 1) * LANES]
        k_head = jnp.where((lane >= 64) == (side == 1), k_pair, 0.0).astype(BF16)
        bit = jnp.left_shift(jnp.int32(1), GROUP * step + i)
        for part in range(2):
            at = slice(part * half, (part + 1) * half)
            s = dot(k_head, q4[at, pair * LANES : (pair + 1) * LANES], NT)
            s = jnp.where((bits_ref[0, :, at] & bit) != 0, s, -1e30)
            top = jnp.max(s, axis=0, keepdims=True)
            e_out[i, :, at] = jnp.exp(s - top).astype(BF16)
        left = jnp.concatenate([v_t[64 * i : 64 * (i + 1), :], ones], axis=0)
        both = dot(left, e_out[i])
        inv = 1.0 / both[64:65, :]
        inv_out[0, i : i + 1, :] = inv
        mix_t_out[64 * i : 64 * (i + 1), :] = (both[:64, :] * inv).astype(BF16)
    mix_out[...] = mix_t_out[...].T


def attn_forward(x, w_query, w_key, w_value, b_query, b_value, bits, row):
    span, width = x.shape
    wide = 64 * GROUP
    steps = width // wide
    col = pl.BlockSpec((span, wide), lambda g: (0, g))
    col_t = pl.BlockSpec((wide, span), lambda g: (g, 0))
    weight = pl.BlockSpec((width, wide), lambda g: (0, g))
    bias = pl.BlockSpec((1, wide), lambda g: (0, g))
    token = jax.ShapeDtypeStruct((span, width), BF16)
    token_t = jax.ShapeDtypeStruct((width, span), BF16)
    return pl.pallas_call(
        attn_kernel,
        grid=(steps,),
        in_specs=[once((span, width))]
        + [weight] * 3
        + [bias] * 2
        + [pl.BlockSpec((1, span, span), lambda g: (row, 0, 0), pipeline_mode=pl.Buffered(1))],
        out_specs=[
            col,
            col,
            col,
            pl.BlockSpec((GROUP, span, span), lambda g: (g, 0, 0)),
            pl.BlockSpec((1, 8, span), lambda g: (g, 0, 0)),
            col_t,
            col,
            col_t,
        ],
        out_shape=[
            token,
            token,
            token,
            jax.ShapeDtypeStruct((HEADS, span, span), BF16),
            jax.ShapeDtypeStruct((steps, 8, span), F32),
            token_t,
            token,
            token_t,
        ],
        compiler_params=params(),
        cost_estimate=cost(14e9),
        name="attn_forward",
    )(x, w_query, w_key, w_value, b_query, b_value, bits)


def norm_forward(values):
    centred = values - jnp.mean(values, axis=-1, keepdims=True)
    inv_scale = lax.rsqrt(jnp.mean(centred * centred, axis=-1, keepdims=True) + EPS)
    return (centred * inv_scale, inv_scale)


def norm_back(grad_normed, normed, inv_scale):
    mean_grad = jnp.mean(grad_normed, axis=-1, keepdims=True)
    mean_cross = jnp.mean(grad_normed * normed, axis=-1, keepdims=True)
    return inv_scale * (grad_normed - mean_grad - normed * mean_cross)


def gelu_parts(values):
    cdf = 0.5 + 0.5 * lax.erf(values * 0.7071067811865476)
    slope = cdf + values * (jnp.exp(-0.5 * values * values) * 0.3989422804014327)
    return values * cdf, slope


def total(values):
    return jnp.sum(values, axis=0, keepdims=True)


def ffn_kernel(*refs):
    (g_ref, x_ref, mix_ref, w_o, w_in, w_out, b_o, gain1, shift1, b_in, b_out, gain2, shift2) = refs[:13]
    (vec_in, wide_in) = refs[13:15]
    (
        h_out,
        first_t_out,
        hidden_out,
        d_inner_out,
        d_outer_t_out,
        d_attn_out,
        d_res_out,
        d_mix_t_out,
        vec_out,
        wide_out,
        wo_s,
        win_s,
        wout_s,
        slope_s,
        sems,
    ) = refs[15:]
    copies = [
        pltpu.make_async_copy(src, dst, sems.at[i])
        for i, (src, dst) in enumerate(((w_o, wo_s), (w_in, win_s), (w_out, wout_s)))
    ]
    for copy in copies:
        copy.start()
    width, inner_width = win_s.shape
    copies[0].wait()
    residual = x_ref[...].astype(F32) + dot(mix_ref[...], wo_s[...]) + b_o[...].astype(F32)
    normed_one, scale_one = norm_forward(residual)
    first = normed_one * gain1[...].astype(F32) + shift1[...].astype(F32)
    first_low = first.astype(BF16)
    first_t_out[...] = first_low.T
    copies[1].wait()
    chunks = [slice(i * width, (i + 1) * width) for i in range(inner_width // width)]
    for at in chunks:
        inner = dot(first_low, win_s[:, at]) + b_in[:, at].astype(F32)
        hidden, slope = gelu_parts(inner)
        hidden_out[:, at] = hidden.astype(BF16)
        slope_s[:, at] = slope.astype(BF16)
    copies[2].wait()
    second = first + dot(hidden_out[...], wout_s[...]) + b_out[...].astype(F32)
    normed_two, scale_two = norm_forward(second)
    result = (normed_two * gain2[...].astype(F32) + shift2[...].astype(F32)).astype(BF16)
    h_out[...] = result
    grad = g_ref[...].astype(F32)
    vec_out[4:5, :] = vec_in[4:5, :] + total(grad * normed_two)
    vec_out[5:6, :] = vec_in[5:6, :] + total(grad)
    d_second = norm_back(grad * gain2[...].astype(F32), normed_two, scale_two)
    d_outer = d_second.astype(BF16)
    d_outer_t_out[...] = d_outer.T
    vec_out[3:4, :] = vec_in[3:4, :] + total(d_outer.astype(F32))
    for at in chunks:
        d_hidden = dot(d_outer, wout_s[at, :], NT)
        d_inner = (d_hidden * slope_s[:, at].astype(F32)).astype(BF16)
        d_inner_out[:, at] = d_inner
        wide_out[0:1, at] = wide_in[0:1, at] + total(d_inner.astype(F32))
    d_first = d_second + dot(d_inner_out[...], win_s[...], NT)
    vec_out[1:2, :] = vec_in[1:2, :] + total(d_first * normed_one)
    vec_out[2:3, :] = vec_in[2:3, :] + total(d_first)
    d_res = norm_back(d_first * gain1[...].astype(F32), normed_one, scale_one)
    d_res_out[...] = d_res
    d_attn = d_res.astype(BF16)
    d_attn_out[...] = d_attn
    vec_out[0:1, :] = vec_in[0:1, :] + total(d_attn.astype(F32))
    d_mix_t_out[...] = dot(wo_s[...], d_attn, NT).astype(BF16)


def ffn_both(grads, x, mixed, weights, vectors, vec_in, wide_in):
    span, width = x.shape
    inner_width = weights[1].shape[1]
    token = jax.ShapeDtypeStruct((span, width), BF16)
    token_t = jax.ShapeDtypeStruct((width, span), BF16)
    wide = jax.ShapeDtypeStruct((span, inner_width), BF16)
    out_shape = [
        token,
        token_t,
        wide,
        wide,
        token_t,
        token,
        jax.ShapeDtypeStruct((span, width), F32),
        token_t,
        jax.ShapeDtypeStruct((8, width), F32),
        jax.ShapeDtypeStruct((8, inner_width), F32),
    ]
    vmem = pl.BlockSpec(memory_space=pltpu.VMEM)
    return pl.pallas_call(
        ffn_kernel,
        in_specs=[vmem] * 3
        + [pl.BlockSpec(memory_space=pl.ANY)] * 3
        + [vmem] * (len(vectors) + 2),
        out_specs=[vmem] * len(out_shape),
        out_shape=out_shape,
        scratch_shapes=[
            pltpu.VMEM(weights[0].shape, BF16),
            pltpu.VMEM(weights[1].shape, BF16),
            pltpu.VMEM(weights[2].shape, BF16),
            pltpu.VMEM((span, inner_width), BF16),
            pltpu.SemaphoreType.DMA((3,)),
        ],
        compiler_params=params(),
        cost_estimate=cost(25e9),
        name="ffn_both",
    )(grads, x, mixed, *weights, *vectors, vec_in, wide_in)


def place_parts(tile_ref, my, keep_ref, send_ref, part, put):
    for p in range(tile_ref.shape[0] // part):
        at = pl.ds(pl.multiple_of((my ^ p) * part, 16), part)
        put(send_ref if p % 2 else keep_ref, p // 2, tile_ref[at, :])


def outer_grad_kernel(my_ref, dot0, dot1, hid0, hid1, keep, send):
    outer = (dot(dot0[...], hid0[...]) + dot(dot1[...], hid1[...])).astype(BF16)
    half = outer.shape[1] // 2
    for refs, core in (((keep, send), 0), ((send, keep), 1)):

        @pl.when(my_ref[0] % 2 == core)
        def _():
            refs[0][0] = outer[:, :half]
            refs[1][0] = outer[:, half:]


def outer_grads(my, d_outer_t, hidden):
    width, span = d_outer_t[0].shape
    steps = hidden[0].shape[1] // width
    half = width // 2
    lhs = pl.BlockSpec((width, span), lambda i, m: (0, 0), pipeline_mode=pl.Buffered(1))
    rhs = pl.BlockSpec((span, width), lambda i, m: (0, (m[0] // 2) ^ i))
    return pl.pallas_call(
        outer_grad_kernel,
        grid_spec=pltpu.PrefetchScalarGridSpec(
            num_scalar_prefetch=1,
            grid=(steps,),
            in_specs=[lhs, lhs, rhs, rhs],
            out_specs=[pl.BlockSpec((1, width, half), lambda i, m: (i, 0, 0))] * 2,
        ),
        out_shape=[jax.ShapeDtypeStruct((steps, width, half), BF16)] * 2,
        compiler_params=params(),
        cost_estimate=cost(10e9),
        name="outer_grads",
    )(my.reshape(1), *d_outer_t, *hidden)


def inner_grad_kernel(my_ref, ft0, ft1, din0, din1, mt0, mt1, da0, da1, keep, send, tile_s):
    last = pl.program_id(0) == pl.num_programs(0) - 1

    @pl.when(jnp.logical_not(last))
    def _():
        tile_s[...] = (dot(ft0[...], din0[...]) + dot(ft1[...], din1[...])).astype(BF16)

    @pl.when(last)
    def _():
        tile_s[...] = (dot(mt0[...], da0[...]) + dot(mt1[...], da1[...])).astype(BF16)

    def put(ref, at, value):
        ref[at, 0] = value

    place_parts(tile_s, my_ref[0], keep, send, keep.shape[2], put)


def inner_grads(my, first_t, d_inner, mix_t, d_attn, groups):
    width, span = first_t[0].shape
    steps = d_inner[0].shape[1] // width
    part = width // groups
    lhs = pl.BlockSpec((width, span), lambda i: (0, 0), pipeline_mode=pl.Buffered(1))
    rhs = pl.BlockSpec((span, width), lambda i: (0, jnp.minimum(i, steps - 1)))
    one = pl.BlockSpec((span, width), lambda i: (0, 0), pipeline_mode=pl.Buffered(1))
    shape = jax.ShapeDtypeStruct((groups // 2, steps + 1, part, width), BF16)
    return pl.pallas_call(
        inner_grad_kernel,
        grid=(steps + 1,),
        in_specs=[SMEM, lhs, lhs, rhs, rhs, lhs, lhs, one, one],
        out_specs=[pl.BlockSpec((groups // 2, 1, part, width), lambda i: (0, i, 0, 0))] * 2,
        out_shape=[shape, shape],
        scratch_shapes=[pltpu.VMEM((width, width), BF16)],
        compiler_params=params(),
        cost_estimate=cost(13e9),
        name="inner_grads",
    )(my.reshape(1), *first_t, *d_inner, *mix_t, *d_attn)


def pair_product_kernel(a0, a1, b0, b1, out):
    out[...] = (dot(a0[...], b0[...]) + dot(a1[...], b1[...])).astype(BF16)


def pair_product(left, right):
    depth = left[0].shape[1]
    rows = left[0].shape[0]
    columns = right[0].shape[1]
    wide = 768
    lhs = pl.BlockSpec((rows, depth), lambda i: (0, 0))
    rhs = pl.BlockSpec((depth, wide), lambda i: (0, i))
    return pl.pallas_call(
        pair_product_kernel,
        grid=(columns // wide,),
        in_specs=[lhs, lhs, rhs, rhs],
        out_specs=pl.BlockSpec((rows, wide), lambda i: (0, i)),
        out_shape=jax.ShapeDtypeStruct((rows, columns), BF16),
        compiler_params=params(),
        cost_estimate=cost(),
        name="pair_product",
    )(*left, *right)


def attn_back_kernel(*refs):
    (q_ref, k_ref, v_ref, e_ref, inv_ref, mix_t, d_mix_t, wq, wk, wv, d_res, vec_in) = refs[:12]
    g_out, dq_out, dk_out, dv_out, vec_out, acc, dq_t = refs[12:]
    step = pl.program_id(0)
    span = q_ref.shape[0]
    k_t = k_ref[...].T
    lane = lax.broadcasted_iota(jnp.int32, (span, LANES), 1)
    blank = jnp.zeros((64, span), BF16)
    for pair in range(GROUP // 2):
        at = slice(pair * LANES, (pair + 1) * LANES)
        q_pair = q_ref[:, at]
        v_pair = v_ref[:, at]
        d_keys = []
        d_values = None
        for side in range(2):
            i = 2 * pair + side
            mine = slice(64 * i, 64 * (i + 1))
            scaled = d_mix_t[mine, :].astype(F32) * inv_ref[0, i : i + 1, :]
            cross = jnp.sum(scaled * mix_t[mine, :].astype(F32), axis=0, keepdims=True)
            scaled = scaled.astype(BF16)
            padded = jnp.concatenate([blank, scaled] if side else [scaled, blank], axis=0)
            d_probs = dot(v_pair, padded)
            d_scores = (e_ref[i].astype(F32) * (d_probs - cross)).astype(BF16)
            d_keys.append(dot(d_scores, q_pair))
            d_value = dot(e_ref[i], padded, NT)
            d_values = d_value if d_values is None else d_values + d_value
            dq_t[mine, :] = dot(k_t[mine, :], d_scores)
        dk_out[:, at] = jnp.where(lane >= 64, d_keys[1], d_keys[0]).astype(BF16)
        dv_out[:, at] = d_values.astype(BF16)
    dq_out[...] = (dq_t[...] * 0.125).T.astype(BF16)
    vec_out[...] = vec_in[...]
    vec_out[0:1, :] += total(dq_out[...].astype(F32))
    vec_out[1:2, :] += total(dv_out[...].astype(F32))
    more = dot(dq_out[...], wq[...], NT) + dot(dk_out[...], wk[...], NT)
    more = more + dot(dv_out[...], wv[...], NT)

    @pl.when(step == 0)
    def _():
        acc[...] = d_res[...] + more

    @pl.when(step > 0)
    def _():
        acc[...] += more

    @pl.when(step == pl.num_programs(0) - 1)
    def _():
        g_out[...] = acc[...].astype(BF16)


def attn_back(q, k, v, e, inv, mix_t, d_mix_t, w_query, w_key, w_value, d_res, vec_in):
    span, width = q.shape
    wide = 64 * GROUP
    steps = width // wide
    col = pl.BlockSpec((span, wide), lambda g: (0, g))
    col_t = pl.BlockSpec((wide, span), lambda g: (g, 0))
    weight = pl.BlockSpec((width, wide), lambda g: (0, g))
    small = pl.BlockSpec((8, wide), lambda g: (0, g))
    token = jax.ShapeDtypeStruct((span, width), BF16)
    return pl.pallas_call(
        attn_back_kernel,
        grid=(steps,),
        in_specs=[
            col,
            col,
            col,
            pl.BlockSpec((GROUP, span, span), lambda g: (g, 0, 0)),
            pl.BlockSpec((1, 8, span), lambda g: (g, 0, 0)),
            col_t,
            col_t,
            weight,
            weight,
            weight,
            once((span, width)),
            small,
        ],
        out_specs=[whole((span, width))] + [col] * 3 + [small],
        out_shape=[token] * 4
        + [jax.ShapeDtypeStruct((8, width), F32)],
        scratch_shapes=[pltpu.VMEM((span, width), F32), pltpu.VMEM((wide, span), F32)],
        compiler_params=params(),
        cost_estimate=cost(17e9),
        name="attn_back",
    )(q, k, v, e, inv, mix_t, d_mix_t, w_query, w_key, w_value, d_res, vec_in)


def attn_grad_kernel(my_ref, xt0, xt1, dq0, dq1, dk0, dk1, dv0, dv1, vec, keep, send, tile_s):
    my = my_ref[0]
    part = tile_s.shape[0] // (2 * keep.shape[0])
    work = (
        (xt0, dq0, xt1, dq1),
        (xt0, dk0, xt1, dk1),
        (xt0, dv0, xt1, dv1),
    )
    for w, (a0, b0, a1, b1) in enumerate(work):
        tile_s[...] = (dot(a0[...], b0[...]) + dot(a1[...], b1[...])).astype(BF16)

        def put(ref, at, value):
            ref[at, w * part : (w + 1) * part, :] = value

        place_parts(tile_s, my, keep, send, part, put)
    low = vec[...].astype(BF16)
    for p in range(keep.shape[0]):
        keep[p, 3 * part :, :] = low
        send[p, 3 * part :, :] = low


def attn_grads_split(my, x_t, d_queries, d_keys, d_values, vec, groups):
    width, span = x_t[0].shape
    part = width // groups
    vmem = pl.BlockSpec(memory_space=pltpu.VMEM)
    shape = jax.ShapeDtypeStruct((groups // 2, 3 * part + 32, width), BF16)
    return pl.pallas_call(
        attn_grad_kernel,
        in_specs=[SMEM] + [vmem] * 9,
        out_specs=[vmem] * 2,
        out_shape=[shape] * 2,
        scratch_shapes=[pltpu.VMEM((width, width), BF16)],
        compiler_params=params(),
        cost_estimate=cost(9.5e9),
        name="attn_grads",
    )(my.reshape(1), *x_t, *d_queries, *d_keys, *d_values, vec)


def swap(values, axis, mask):
    size = lax.axis_size(axis)
    return lax.ppermute(values, axis, [(i, i ^ mask) for i in range(size)])


def added(left, right):
    return (left.astype(F32) + right.astype(F32)).astype(BF16)


def exchange(values, axis, groups=None):
    return lax.all_to_all(values, axis, 0, 0, tiled=True, axis_index_groups=groups)


def by_core(blocks):
    turned = jnp.take(blocks, jnp.arange(blocks.shape[0]) ^ lax.axis_index("dp"), axis=0)
    return turned[0::2], turned[1::2]


class ChipSum:
    def __init__(self, keep, send):
        bits = list(range(1, lax.axis_size("dp").bit_length() - 1))
        got = swap(send, "dp", 1)
        half = keep.shape[1] // 2
        alive = list(range(keep.shape[0]))
        self.parts = [
            (keep[:, :half], got[:, :half], alive, bits),
            (keep[:, half:], got[:, half:], alive, bits[::-1]),
        ]

    def advance(self):
        ready, parts = [], []
        for keep, got, alive, bits in self.parts:
            held = added(keep, got)
            if bits:
                bit = bits[0] - 1
                stay = [n for n, p in enumerate(alive) if not (p >> bit) & 1]
                go = [n for n, p in enumerate(alive) if (p >> bit) & 1]
                keep = jnp.stack([held[n] for n in stay])
                send = jnp.stack([held[n] for n in go])
                ready += [keep, send]
                got = swap(send, "dp", 2 << bit)
                parts.append((keep, got, [alive[n] for n in stay], bits[1:]))
            else:
                ready.append(held)
                parts.append(held[0])
        self.parts = parts
        return ready

    def finish(self):
        while isinstance(self.parts[0], tuple):
            self.advance()
        return jnp.concatenate(self.parts, axis=0)


class LineSum:
    def __init__(self, rows):
        place = lax.axis_index("blk")
        size = lax.axis_size("blk")
        self.bits = [1 << b for b in range(size.bit_length() - 1)]
        self.held = rows
        self.mine = [(place // bit) % 2 for bit in self.bits]
        self.step = 0

    def start(self):
        held = self.held.reshape((2, -1) + self.held.shape[1:])
        mine = self.mine[self.step]
        self.keep = lax.dynamic_index_in_dim(held, mine, 0, keepdims=False)
        send = lax.dynamic_index_in_dim(held, 1 - mine, 0, keepdims=False)
        self.got = swap(send, "blk", self.bits[self.step])
        self.step += 1
        return self.keep, send

    def add(self):
        self.held = added(self.keep, self.got)
        return self.held

    def gather(self):
        pieces = self.held[None]
        for bit in self.bits[::-1]:
            pieces = jnp.concatenate([pieces, swap(pieces, "blk", bit)], axis=0)
        return pieces

    def finish(self):
        while self.step < len(self.bits):
            self.start()
            self.add()
        return self.gather()


def row_of(place, piece):
    return (((place % 2) ^ (piece // 2)) * 2) + (((place // 2) % 2) ^ (piece % 2))


def line_join(pieces):
    place = lax.axis_index("blk")
    order = row_of(place, jnp.arange(pieces.shape[0]))
    return jnp.take(pieces, jnp.argsort(order), axis=0).reshape((-1,) + pieces.shape[2:])


def join(place, pieces, rows_ref):
    share = pieces.shape[1]
    for n in range(pieces.shape[0]):
        at = pl.ds(pl.multiple_of(row_of(place, n) * share, 8), share)
        rows_ref[at, :] = pieces[n].astype(F32)


def outer_result_kernel(place_ref, pieces, out, rows_s):
    join(place_ref[0], pieces, rows_s)
    out[...] = rows_s[...].T


def outer_result(place, pieces):
    rows, half = pieces.shape[0] * pieces.shape[1], pieces.shape[2]
    vmem = pl.BlockSpec(memory_space=pltpu.VMEM)
    return pl.pallas_call(
        outer_result_kernel,
        in_specs=[SMEM, vmem],
        out_specs=vmem,
        out_shape=jax.ShapeDtypeStruct((half, rows), F32),
        scratch_shapes=[pltpu.VMEM((rows, half), F32)],
        compiler_params=params(),
        cost_estimate=cost(2e9),
        name="outer_result",
    )(place.reshape(1), pieces)


def inner_result_kernel(place_ref, pieces, inner_out, attn_out, rows_s):
    join(place_ref[0], pieces, rows_s)
    part, wide = inner_out.shape
    width = rows_s.shape[1]
    count = wide // width
    for i in range(count):
        inner_out[:, i * width : (i + 1) * width] = rows_s[i * part : (i + 1) * part, :]
    attn_out[...] = rows_s[count * part :, :]


def inner_result(place, pieces, part):
    rows, width = pieces.shape[0] * pieces.shape[1], pieces.shape[2]
    vmem = pl.BlockSpec(memory_space=pltpu.VMEM)
    return pl.pallas_call(
        inner_result_kernel,
        in_specs=[SMEM, vmem],
        out_specs=[vmem] * 2,
        out_shape=[
            jax.ShapeDtypeStruct((part, (rows // part - 1) * width), F32),
            jax.ShapeDtypeStruct((part, width), F32),
        ],
        scratch_shapes=[pltpu.VMEM((rows, width), F32)],
        compiler_params=params(),
        cost_estimate=cost(2e9),
        name="inner_result",
    )(place.reshape(1), pieces)


def late_kernel(lanes_ref, pieces, *outs):
    late = outs[-1]
    join(lanes_ref[3], pieces, late)
    part = outs[0].shape[0]
    for w in range(3):
        outs[w][...] = late[w * part : (w + 1) * part, :]
    vec = late[3 * part :, :].astype(BF16)
    width = vec.shape[1]
    size = outs[3].shape[1]

    def picked(start, count):
        lanes = -(-count // LANES) * LANES
        source = lax.broadcasted_iota(jnp.int32, (width, lanes), 0)
        target = lax.broadcasted_iota(jnp.int32, (width, lanes), 1)
        return jnp.where(source == target + start, 1.0, 0.0).astype(BF16)

    narrow = dot(vec, picked(lanes_ref[0], size))
    for n in range(8):
        outs[3 + n][...] = narrow[n : n + 1, :size]
    count = outs[11].shape[1]
    broad = dot(vec, picked(lanes_ref[1], count))
    row = lax.broadcasted_iota(jnp.int32, broad.shape, 0)
    broad = jnp.where(row == lanes_ref[2], broad, 0.0)
    outs[11][...] = total(broad)[:, :count]


def late_results(place, pieces, groups, inner_width):
    rows, width = pieces.shape[0] * pieces.shape[1], pieces.shape[2]
    part = (rows - 32) // 3
    size = width // groups
    count = inner_width // groups
    my = lax.axis_index("dp")
    start = my * count
    lanes = jnp.stack([my * size, start % width, 8 + start // width, place]).astype(jnp.int32)
    vmem = pl.BlockSpec(memory_space=pltpu.VMEM)
    shapes = (
        [jax.ShapeDtypeStruct((part, width), F32)] * 3
        + [jax.ShapeDtypeStruct((1, size), F32)] * 8
        + [jax.ShapeDtypeStruct((1, count), F32)]
    )
    outs = pl.pallas_call(
        late_kernel,
        in_specs=[SMEM, vmem],
        out_specs=[vmem] * len(shapes),
        out_shape=shapes,
        scratch_shapes=[pltpu.VMEM((rows, width), F32)],
        compiler_params=params(),
        cost_estimate=cost(3e9),
        name="late_results",
    )(lanes, pieces)
    return list(outs[:3]), [value.reshape(-1) for value in outs[3:]]


def spread_kernel(*refs):
    out = refs[-1]
    for r, piece in enumerate(refs[:-1]):
        out[:, r] = piece[...].astype(out.dtype)


def spread(pieces, dtype):
    micro, blk_len, width = pieces[0].shape
    rows = len(pieces)
    return pl.pallas_call(
        spread_kernel,
        grid=(micro,),
        in_specs=[pl.BlockSpec((1, blk_len, width), lambda m: (m, 0, 0))] * rows,
        out_specs=pl.BlockSpec((1, rows, blk_len, width), lambda m: (m, 0, 0, 0)),
        out_shape=jax.ShapeDtypeStruct((micro, rows, blk_len, width), dtype),
        compiler_params=params(),
        cost_estimate=cost(3e9),
        name="spread",
    )(*pieces)


def local(
    hidden_in,
    seq_lengths,
    dam_mask,
    w_query,
    b_query,
    w_key,
    w_value,
    b_value,
    w_attn_out,
    b_attn_out,
    gain_attn,
    shift_attn,
    w_inner,
    b_inner,
    w_outer,
    b_outer,
    gain_ffn,
    shift_ffn,
    grad_out,
):
    micro, rows, blk_len, width = hidden_in.shape
    cycle = lax.axis_size("blk")
    groups = lax.axis_size("dp")
    inner_width = w_inner.shape[1]
    place = lax.axis_index("blk")
    my = lax.axis_index("dp")

    def whole_row(values, row):
        return exchange(values[:, row], "blk").reshape(-1, width)

    def home(values):
        return exchange(values.reshape(cycle, blk_len, width), "blk")

    def flat(vector):
        return vector.reshape(1, -1)

    tokens = [whole_row(hidden_in, 0)]
    lengths = lax.dynamic_index_in_dim(seq_lengths, place, 0, keepdims=False)
    bits = mask_bits(lengths, dam_mask)
    tokens += [whole_row(after(hidden_in, bits), r) for r in range(1, rows)]
    vectors = [
        flat(v)
        for v in (b_attn_out, gain_attn, shift_attn, b_inner, b_outer, gain_ffn, shift_ffn)
    ]
    ahead = []
    for r in range(rows):
        if r:
            tokens[r] = after(tokens[r], ahead[-1][0])
        ahead.append(
            attn_forward(tokens[r], w_query, w_key, w_value, flat(b_query), flat(b_value), bits, r)
        )
    grads = [whole_row(after(grad_out, ahead[r][0]), r) for r in range(rows)]
    vec = jnp.zeros((8, width), F32)
    wide = jnp.zeros((8, inner_width), F32)
    kept = []
    results = []
    for r in range(rows):
        x, mixed = tokens[r], ahead[r][6]
        if r == 0:
            x = after(x, ahead[-1][0])
        result = ffn_both(
            grads[r], x, mixed, (w_attn_out, w_inner, w_outer), vectors, vec, wide
        )
        results.append(home(result[0]))
        vec, wide = result[-2:]
        kept.append((ahead[r], result[1:-2]))
    hidden_out = spread(results, BF16)

    first_t = [k[1][0] for k in kept]
    hidden = [k[1][1] for k in kept]
    d_inner = [k[1][2] for k in kept]
    d_outer_t = [k[1][3] for k in kept]
    d_attn = [k[1][4] for k in kept]
    part = width // groups
    aligned = part % 16 == 0 and groups == 2 * (inner_width // width)
    mix_t = [k[0][5] for k in kept]
    if aligned:
        hidden = [after(hidden[0], results[0])] + hidden[1:]
        outer = outer_grads(my, d_outer_t, hidden)
        d_inner = [after(d_inner[0], outer)] + d_inner[1:]
        inner = inner_grads(my, first_t, d_inner, mix_t, d_attn, groups)
    else:
        outer = pair_product(d_outer_t, hidden)
        outer = by_core(outer.reshape(width, groups, -1).transpose(1, 2, 0))
        inner = pair_product(first_t, d_inner).reshape(groups, part, inner_width)
        attn = pair_product(mix_t, d_attn).reshape(groups, part, width)
        pieces = jnp.split(inner, inner_width // width, axis=2) + [attn]
        inner = by_core(jnp.concatenate(pieces, axis=1))
    inner = [value.reshape(value.shape[0], -1, width) for value in inner]
    outer_sum = ChipSum(*outer)
    inner_sum = ChipSum(*inner)
    ready = (results[1:], inner, outer_sum.advance())

    vec_two = jnp.zeros((8, width), F32)
    back = []
    returned = []
    for r in range(rows):
        q, k, v, e, inv, mix_t = kept[r][0][:6]
        d_res, d_mix_t = kept[r][1][5:7]
        d_res = after(d_res, ready)
        outs = attn_back(q, k, v, e, inv, mix_t, d_mix_t, w_query, w_key, w_value, d_res, vec_two)
        returned.append(home(outs[0]))
        vec_two = outs[-1]
        back.append(outs[1:-1])
        if r == 0:
            ready = (outer_sum.advance(), inner_sum.advance())

    small = jnp.concatenate(
        [vec_two[:2], vec[:6], wide[0].reshape(-1, width), jnp.zeros((20, width), F32)], axis=0
    )
    small = after(small, returned[0], outer_sum.advance(), inner_sum.advance())
    outer_line = LineSum(outer_sum.finish())
    outer_line.start()
    x_t = [k[0][7] for k in kept]
    d_queries, d_keys, d_values = [[b[n] for b in back] for n in range(3)]
    if aligned:
        late = attn_grads_split(my, x_t, d_queries, d_keys, d_values, small, groups)
    else:
        late = [
            pair_product(x_t, d_queries),
            pair_product(x_t, d_keys),
            pair_product(x_t, d_values),
        ]
        late = [value.reshape(groups, part, width) for value in late]
        late.append(jnp.broadcast_to(small.astype(BF16), (groups, 32, width)))
        late = by_core(jnp.concatenate(late, axis=1))
    late_sum = ChipSum(*late)
    grad_in = spread(returned, F32)
    outer_line.add()
    outer = outer_line.finish()
    inner = LineSum(inner_sum.finish()).finish()
    late = LineSum(late_sum.finish()).finish()
    if aligned:
        g_outer = outer_result(place, outer)
        g_inner, g_attn = inner_result(place, inner, part)
        mats, vecs = late_results(place, late, groups, inner_width)
    else:
        g_outer = line_join(outer).astype(F32)
        inner = line_join(inner).astype(F32)
        late = line_join(late)
        g_inner = jnp.concatenate(
            [inner[i * part : (i + 1) * part] for i in range(inner_width // width)], axis=1
        )
        g_attn = inner[part * (inner_width // width) :]
        mats = [late[w * part : (w + 1) * part].astype(F32) for w in range(3)]
        sums = late[3 * part :].astype(F32)
        vecs = [
            lax.dynamic_slice_in_dim(sums[n], my * part, part, 0) for n in range(8)
        ]
        count = inner_width // groups
        vecs.append(lax.dynamic_slice_in_dim(sums[8:12].reshape(-1), my * count, count, 0))
    g_query, g_key, g_value = mats
    s_query, s_value, s_attn, s_gain, s_shift, s_outer, s_gain2, s_shift2, s_inner = vecs
    return (
        hidden_out,
        grad_in,
        g_query,
        s_query,
        g_key,
        g_value,
        s_value,
        g_attn,
        s_attn,
        s_gain,
        s_shift,
        g_inner,
        s_inner,
        g_outer,
        s_outer,
        s_gain2,
        s_shift2,
    )


def solution(mesh):
    placed = (P(None, "dp", "blk", None), P(None, "dp", None)) + (P(),) * 16
    placed = placed + (P(None, "dp", "blk", None),)
    return jax.shard_map(
        local,
        mesh=mesh,
        in_specs=placed,
        out_specs=(
            P(None, "dp", "blk", None),
            P(None, "dp", "blk", None),
            P("dp", None),
            P("dp"),
            P("dp", None),
            P("dp", None),
            P("dp"),
            P("dp", None),
            P("dp"),
            P("dp"),
            P("dp"),
            P("dp", None),
            P("dp"),
            P("dp", None),
            P("dp"),
            P("dp"),
            P("dp"),
        ),
        check_vma=False,
    )
```

```python
import functools

import jax
import jax.numpy as jnp
from jax import lax
from jax.experimental import pallas as pl
from jax.experimental.pallas import tpu as pltpu
from jax.sharding import PartitionSpec as P

HEADS = 12


EPS = 1e-12
F32 = jnp.float32
BF16 = jnp.bfloat16
NN = ((1,), (0,))
NT = ((1,), (1,))
LIMIT = 56 * 1024 * 1024
GROUP = 4
LANES = 128


def dot(left, right, dims=NN):
    return lax.dot_general(left, right, (dims, ((), ())), preferred_element_type=F32)


def params():
    return pltpu.CompilerParams(vmem_limit_bytes=LIMIT)


SCALE = 1.0


def cost(flops=1e9):
    return pl.CostEstimate(flops=int(SCALE * flops), bytes_accessed=1000, transcendentals=0)


def after(value, *others):
    return lax.optimization_barrier((value, others))[0]


def whole(shape):
    return pl.BlockSpec(shape, lambda *_: (0,) * len(shape))


def once(shape):
    return pl.BlockSpec(shape, lambda *_: (0,) * len(shape), pipeline_mode=pl.Buffered(1))


SMEM = pl.BlockSpec(memory_space=pltpu.SMEM)


def mask_kernel(chunks, len_ref, dam_ref, bias_ref, low_ref, high_ref, bits_ref):
    step = pl.program_id(0)
    chunk = dam_ref.shape[1]
    span = dam_ref.shape[2]
    later = step - chunks
    groups = HEADS // GROUP

    @pl.when(step < chunks)
    def _():
        low = dam_ref[0]
        for h in range(1, 8):
            low = low + (dam_ref[h] << h)
        high = dam_ref[8]
        for h in range(9, HEADS):
            high = high + (dam_ref[h] << (h - 8))
        at = pl.ds(pl.multiple_of(step * chunk, chunk), chunk)
        low_ref[at, :] = low.astype(F32).astype(BF16)
        high_ref[at, :] = high.astype(F32).astype(BF16)

    @pl.when((later >= 0) & (later % groups == 0))
    def _():
        row = later // groups
        first = len_ref[row, 0]
        second = first + len_ref[row, 1]

        def segment(at_place):
            one = jnp.where(at_place >= first, 1, 0)
            return one + jnp.where(at_place >= second, 1, 0)

        down = lax.broadcasted_iota(jnp.int32, (span, span), 0)
        across = lax.broadcasted_iota(jnp.int32, (span, span), 1)
        inside = (
            down
            - jnp.where(down >= first, first, 0)
            - jnp.where(down >= second, second - first, 0)
        )
        pick = jnp.where(inside == across, 1.0, 0.0).astype(BF16)

        def moved(table):
            one = dot(pick, table, NT).astype(BF16)
            return dot(one, pick, NT).astype(jnp.int32)

        bits = moved(low_ref[...]) + (moved(high_ref[...]) << 8)
        bits_ref[...] = jnp.where(segment(down) == segment(across), bits, 0)

    @pl.when(later >= 0)
    def _():
        for n in range(GROUP):
            bit = jnp.left_shift(jnp.int32(1), GROUP * (later % groups) + n)
            bias_ref[0, n] = jnp.where((bits_ref[...] & bit) != 0, 0.0, -1e30).astype(BF16)


def mask_bias(lengths, dam_mask):
    heads, span, _ = dam_mask.shape
    rows = lengths.shape[0]
    chunk = 64
    chunks = span // chunk
    groups = heads // GROUP

    def placed(i):
        later = jnp.maximum(i - chunks, 0)
        return (later // groups, later % groups, 0, 0)

    return pl.pallas_call(
        functools.partial(mask_kernel, chunks),
        grid=(chunks + rows * groups,),
        in_specs=[
            SMEM,
            pl.BlockSpec((heads, chunk, span), lambda i: (0, jnp.minimum(i, chunks - 1), 0)),
        ],
        out_specs=pl.BlockSpec((1, GROUP, span, span), placed),
        out_shape=jax.ShapeDtypeStruct((rows, heads, span, span), BF16),
        scratch_shapes=[pltpu.VMEM((span, span), BF16)] * 2 + [pltpu.VMEM((span, span), jnp.int32)],
        compiler_params=params(),
        cost_estimate=cost(15e9),
        name="mask_bias",
    )(lengths, dam_mask)


def attn_kernel(
    x_ref, wq, wk, wv, bq, bv, bias_ref, q_out, k_out, v_out, e_out, inv_out, mix_out, x_out,
    mix_t_out, x_t_out
):
    step = pl.program_id(1)
    wide = wq.shape[1]
    width = x_ref.shape[3]
    span = x_ref.shape[0] * x_ref.shape[2]
    x = x_ref[...].reshape(span, width)
    cols = pl.ds(pl.multiple_of(step * wide, wide), wide)
    x_cols = x_ref[:, :, :, cols].reshape(span, wide)
    x_out[...] = x_cols
    x_t_out[...] = x_cols.T
    q4 = ((dot(x, wq[...]) + bq[...].astype(F32)) * 0.125).astype(BF16)
    k4 = dot(x, wk[...])
    v4 = (dot(x, wv[...]) + bv[...].astype(F32)).astype(BF16)
    q_out[0] = q4
    k_out[0] = k4.astype(BF16)
    v_out[0] = v4
    v_t = v4.T
    lane = lax.broadcasted_iota(jnp.int32, (span, LANES), 1)
    ones = jnp.ones((16, span), BF16)
    half = span // 2
    for i in range(GROUP):
        pair, side = i // 2, i % 2
        k_pair = k4[:, pair * LANES : (pair + 1) * LANES]
        k_head = jnp.where((lane >= 64) == (side == 1), k_pair, 0.0).astype(BF16)
        for part in range(2):
            at = slice(part * half, (part + 1) * half)
            s = dot(k_head, q4[at, pair * LANES : (pair + 1) * LANES], NT)
            s = s + bias_ref[0, i, :, at].astype(F32)
            top = jnp.max(s, axis=0, keepdims=True)
            e_out[0, i, :, at] = jnp.exp(s - top).astype(BF16)
        left = jnp.concatenate([v_t[64 * i : 64 * (i + 1), :], ones], axis=0)
        both = dot(left, e_out[0, i])
        inv = 1.0 / both[64:65, :]
        inv_out[0, 0, i : i + 1, :] = inv
        mix_t_out[64 * i : 64 * (i + 1), :] = (both[:64, :] * inv).astype(BF16)
    mix_out[...] = mix_t_out[...].T


def attn_forward(x, w_query, w_key, w_value, b_query, b_value, bias):
    cycle, rows, blk_len, width = x.shape
    span = cycle * blk_len
    wide = 64 * GROUP
    steps = width // wide
    head = pl.BlockSpec((1, span, wide), lambda r, g: (r, 0, g))
    col = pl.BlockSpec((span, wide), lambda r, g: (r, g))
    col_t = pl.BlockSpec((wide, span), lambda r, g: (g, r))
    weight = pl.BlockSpec((width, wide), lambda r, g: (0, g))
    small = pl.BlockSpec((1, wide), lambda r, g: (0, g))
    square = pl.BlockSpec((1, GROUP, span, span), lambda r, g: (r, g, 0, 0))
    heads = jax.ShapeDtypeStruct((rows, span, width), BF16)
    token = jax.ShapeDtypeStruct((rows * span, width), BF16)
    token_t = jax.ShapeDtypeStruct((width, rows * span), BF16)
    return pl.pallas_call(
        attn_kernel,
        grid=(rows, steps),
        in_specs=[pl.BlockSpec((cycle, 1, blk_len, width), lambda r, g: (0, r, 0, 0))]
        + [weight] * 3
        + [small] * 2
        + [square],
        out_specs=[
            head,
            head,
            head,
            square,
            pl.BlockSpec((1, 1, 8, span), lambda r, g: (r, g, 0, 0)),
            col,
            col,
            col_t,
            col_t,
        ],
        out_shape=[
            heads,
            heads,
            heads,
            jax.ShapeDtypeStruct((rows, HEADS, span, span), BF16),
            jax.ShapeDtypeStruct((rows, steps, 8, span), F32),
            token,
            token,
            token_t,
            token_t,
        ],
        compiler_params=params(),
        cost_estimate=cost(26e9),
        name="attn_forward",
    )(x, w_query, w_key, w_value, b_query, b_value, bias)


def norm_forward(values):
    centred = values - jnp.mean(values, axis=-1, keepdims=True)
    inv_scale = lax.rsqrt(jnp.mean(centred * centred, axis=-1, keepdims=True) + EPS)
    return (centred * inv_scale, inv_scale)


def norm_back(grad_normed, normed, inv_scale):
    mean_grad = jnp.mean(grad_normed, axis=-1, keepdims=True)
    mean_cross = jnp.mean(grad_normed * normed, axis=-1, keepdims=True)
    return inv_scale * (grad_normed - mean_grad - normed * mean_cross)


def gelu_parts(values):
    cdf = 0.5 + 0.5 * lax.erf(values * 0.7071067811865476)
    slope = cdf + values * (jnp.exp(-0.5 * values * values) * 0.3989422804014327)
    return values * cdf, slope


def total(values):
    return jnp.sum(values, axis=0, keepdims=True)


def ffn_kernel(*refs):
    (g_ref, x_ref, mix_ref, w_o, w_in, w_out, b_o, gain1, shift1, b_in, b_out, gain2, shift2) = refs[:13]
    (vec_in, wide_in) = refs[13:15]
    (
        h_out,
        first_t_out,
        hidden_out,
        d_inner_out,
        d_outer_t_out,
        d_attn_out,
        d_res_out,
        d_mix_t_out,
        vec_out,
        wide_out,
        wo_s,
        win_s,
        wout_s,
        slope_s,
        sems,
    ) = refs[15:]
    copies = [
        pltpu.make_async_copy(src, dst, sems.at[i])
        for i, (src, dst) in enumerate(((w_o, wo_s), (w_in, win_s), (w_out, wout_s)))
    ]
    for copy in copies:
        copy.start()
    width, inner_width = win_s.shape
    copies[0].wait()
    residual = x_ref[...].astype(F32) + dot(mix_ref[...], wo_s[...]) + b_o[...].astype(F32)
    normed_one, scale_one = norm_forward(residual)
    first = normed_one * gain1[...].astype(F32) + shift1[...].astype(F32)
    first_low = first.astype(BF16)
    first_t_out[...] = first_low.T
    copies[1].wait()
    chunks = [slice(i * width, (i + 1) * width) for i in range(inner_width // width)]
    for at in chunks:
        inner = dot(first_low, win_s[:, at]) + b_in[:, at].astype(F32)
        hidden, slope = gelu_parts(inner)
        hidden_out[:, at] = hidden.astype(BF16)
        slope_s[:, at] = slope.astype(BF16)
    copies[2].wait()
    second = first + dot(hidden_out[...], wout_s[...]) + b_out[...].astype(F32)
    normed_two, scale_two = norm_forward(second)
    result = (normed_two * gain2[...].astype(F32) + shift2[...].astype(F32)).astype(BF16)
    h_out[...] = result
    grad = g_ref[...].astype(F32)
    vec_out[4:5, :] = vec_in[4:5, :] + total(grad * normed_two)
    vec_out[5:6, :] = vec_in[5:6, :] + total(grad)
    d_second = norm_back(grad * gain2[...].astype(F32), normed_two, scale_two)
    d_outer = d_second.astype(BF16)
    d_outer_t_out[...] = d_outer.T
    vec_out[3:4, :] = vec_in[3:4, :] + total(d_outer.astype(F32))
    for at in chunks:
        d_hidden = dot(d_outer, wout_s[at, :], NT)
        d_inner = (d_hidden * slope_s[:, at].astype(F32)).astype(BF16)
        d_inner_out[:, at] = d_inner
        wide_out[0:1, at] = wide_in[0:1, at] + total(d_inner.astype(F32))
    d_first = d_second + dot(d_inner_out[...], win_s[...], NT)
    vec_out[1:2, :] = vec_in[1:2, :] + total(d_first * normed_one)
    vec_out[2:3, :] = vec_in[2:3, :] + total(d_first)
    d_res = norm_back(d_first * gain1[...].astype(F32), normed_one, scale_one)
    d_res_out[...] = d_res
    d_attn = d_res.astype(BF16)
    d_attn_out[...] = d_attn
    vec_out[0:1, :] = vec_in[0:1, :] + total(d_attn.astype(F32))
    d_mix_t_out[...] = dot(wo_s[...], d_attn, NT).astype(BF16)


def ffn_both(row, grads, x, mixed, weights, vectors, vec_in, wide_in):
    span, width = grads.shape
    inner_width = weights[1].shape[1]
    token = jax.ShapeDtypeStruct((span, width), BF16)
    token_t = jax.ShapeDtypeStruct((width, span), BF16)
    wide = jax.ShapeDtypeStruct((span, inner_width), BF16)
    out_shape = [
        token,
        token_t,
        wide,
        wide,
        token_t,
        token,
        jax.ShapeDtypeStruct((span, width), F32),
        token_t,
        jax.ShapeDtypeStruct((8, width), F32),
        jax.ShapeDtypeStruct((8, inner_width), F32),
    ]
    mine = pl.BlockSpec((span, width), lambda i: (row, 0), pipeline_mode=pl.Buffered(1))
    return pl.pallas_call(
        ffn_kernel,
        grid=(1,),
        in_specs=[once((span, width)), mine, mine]
        + [pl.BlockSpec(memory_space=pl.ANY)] * 3
        + [once(v.shape) for v in (*vectors, vec_in, wide_in)],
        out_specs=[once(o.shape) for o in out_shape],
        out_shape=out_shape,
        scratch_shapes=[
            pltpu.VMEM(weights[0].shape, BF16),
            pltpu.VMEM(weights[1].shape, BF16),
            pltpu.VMEM(weights[2].shape, BF16),
            pltpu.VMEM((span, inner_width), BF16),
            pltpu.SemaphoreType.DMA((3,)),
        ],
        compiler_params=params(),
        cost_estimate=cost(25e9),
        name="ffn_both",
    )(grads, x, mixed, *weights, *vectors, vec_in, wide_in)


def place_parts(tile_ref, my, keep_ref, send_ref, part, put):
    for p in range(tile_ref.shape[0] // part):
        at = pl.ds(pl.multiple_of((my ^ p) * part, 16), part)
        put(send_ref if p % 2 else keep_ref, p // 2, tile_ref[at, :])


def outer_grad_kernel(my_ref, dot0, dot1, hid0, hid1, keep, send):
    outer = (dot(dot0[...], hid0[...]) + dot(dot1[...], hid1[...])).astype(BF16)
    half = outer.shape[1] // 2
    for refs, core in (((keep, send), 0), ((send, keep), 1)):

        @pl.when(my_ref[0] % 2 == core)
        def _():
            refs[0][0] = outer[:, :half]
            refs[1][0] = outer[:, half:]


def outer_grads(my, d_outer_t, hidden):
    width, span = d_outer_t[0].shape
    steps = hidden[0].shape[1] // width
    half = width // 2
    lhs = pl.BlockSpec((width, span), lambda i, m: (0, 0), pipeline_mode=pl.Buffered(1))
    rhs = pl.BlockSpec((span, width), lambda i, m: (0, (m[0] // 2) ^ i))
    return pl.pallas_call(
        outer_grad_kernel,
        grid_spec=pltpu.PrefetchScalarGridSpec(
            num_scalar_prefetch=1,
            grid=(steps,),
            in_specs=[lhs, lhs, rhs, rhs],
            out_specs=[pl.BlockSpec((1, width, half), lambda i, m: (i, 0, 0))] * 2,
        ),
        out_shape=[jax.ShapeDtypeStruct((steps, width, half), BF16)] * 2,
        compiler_params=params(),
        cost_estimate=cost(10e9),
        name="outer_grads",
    )(my.reshape(1), *d_outer_t, *hidden)


def inner_grad_kernel(my_ref, ft0, ft1, din0, din1, mt0, mt1, da0, da1, keep, send, tile_s):
    last = pl.program_id(0) == pl.num_programs(0) - 1

    @pl.when(jnp.logical_not(last))
    def _():
        tile_s[...] = (dot(ft0[...], din0[...]) + dot(ft1[...], din1[...])).astype(BF16)

    @pl.when(last)
    def _():
        tile_s[...] = (dot(mt0[...], da0[...]) + dot(mt1[...], da1[...])).astype(BF16)

    def put(ref, at, value):
        ref[at, 0] = value

    place_parts(tile_s, my_ref[0], keep, send, keep.shape[2], put)


def inner_grads(my, first_t, d_inner, mix_t, d_attn, groups):
    width, span = first_t[0].shape
    steps = d_inner[0].shape[1] // width
    part = width // groups
    lhs = pl.BlockSpec((width, span), lambda i: (0, 0), pipeline_mode=pl.Buffered(1))
    rhs = pl.BlockSpec((span, width), lambda i: (0, jnp.minimum(i, steps - 1)))
    one = pl.BlockSpec((span, width), lambda i: (0, 0), pipeline_mode=pl.Buffered(1))
    other = pl.BlockSpec((width, span), lambda i: (0, 1), pipeline_mode=pl.Buffered(1))
    shape = jax.ShapeDtypeStruct((groups // 2, steps + 1, part, width), BF16)
    return pl.pallas_call(
        inner_grad_kernel,
        grid=(steps + 1,),
        in_specs=[SMEM, lhs, lhs, rhs, rhs, lhs, other, one, one],
        out_specs=[pl.BlockSpec((groups // 2, 1, part, width), lambda i: (0, i, 0, 0))] * 2,
        out_shape=[shape, shape],
        scratch_shapes=[pltpu.VMEM((width, width), BF16)],
        compiler_params=params(),
        cost_estimate=cost(13e9),
        name="inner_grads",
    )(my.reshape(1), *first_t, *d_inner, mix_t, mix_t, *d_attn)


def pair_product_kernel(a0, a1, b0, b1, out):
    out[...] = (dot(a0[...], b0[...]) + dot(a1[...], b1[...])).astype(BF16)


def pair_product(left, right):
    depth = left[0].shape[1]
    rows = left[0].shape[0]
    columns = right[0].shape[1]
    wide = 768
    lhs = pl.BlockSpec((rows, depth), lambda i: (0, 0))
    rhs = pl.BlockSpec((depth, wide), lambda i: (0, i))
    return pl.pallas_call(
        pair_product_kernel,
        grid=(columns // wide,),
        in_specs=[lhs, lhs, rhs, rhs],
        out_specs=pl.BlockSpec((rows, wide), lambda i: (0, i)),
        out_shape=jax.ShapeDtypeStruct((rows, columns), BF16),
        compiler_params=params(),
        cost_estimate=cost(),
        name="pair_product",
    )(*left, *right)


def attn_back_kernel(
    q_ref, k_ref, v_ref, e_ref, inv_ref, mix_t, d_mix_t, wq, wk, wv, d_res,
    g_out, out, vec_out,
    acc, dq_t,
):
    step = pl.program_id(0)
    span = q_ref.shape[1]
    k_t = k_ref[0].T
    lane = lax.broadcasted_iota(jnp.int32, (span, LANES), 1)
    blank = jnp.zeros((64, span), BF16)
    for pair in range(GROUP // 2):
        at = slice(pair * LANES, (pair + 1) * LANES)
        q_pair = q_ref[0, :, at]
        v_pair = v_ref[0, :, at]
        d_keys = []
        d_values = None
        for side in range(2):
            i = 2 * pair + side
            mine = slice(64 * i, 64 * (i + 1))
            scaled = d_mix_t[mine, :].astype(F32) * inv_ref[0, 0, i : i + 1, :]
            cross = jnp.sum(scaled * mix_t[mine, :].astype(F32), axis=0, keepdims=True)
            scaled = scaled.astype(BF16)
            padded = jnp.concatenate([blank, scaled] if side else [scaled, blank], axis=0)
            d_probs = dot(v_pair, padded)
            d_scores = (e_ref[0, i].astype(F32) * (d_probs - cross)).astype(BF16)
            d_keys.append(dot(d_scores, q_pair))
            d_value = dot(e_ref[0, i], padded, NT)
            d_values = d_value if d_values is None else d_values + d_value
            dq_t[mine, :] = dot(k_t[mine, :], d_scores)
        out[1, :, at] = jnp.where(lane >= 64, d_keys[1], d_keys[0]).astype(BF16)
        out[2, :, at] = d_values.astype(BF16)
    out[0] = (dq_t[...] * 0.125).T.astype(BF16)
    vec_out[0:1, :] = total(out[0].astype(F32))
    vec_out[1:2, :] = total(out[2].astype(F32))
    more = dot(out[0], wq[...], NT) + dot(out[1], wk[...], NT) + dot(out[2], wv[...], NT)

    @pl.when(step == 0)
    def _():
        acc[...] = d_res[...] + more

    @pl.when(step > 0)
    def _():
        acc[...] += more

    @pl.when(step == pl.num_programs(0) - 1)
    def _():
        g_out[...] = acc[...].astype(BF16).reshape(g_out.shape)


def attn_back(row, q, k, v, e, inv, mix_t, d_mix_t, w_query, w_key, w_value, d_res, cycle):
    rows, span, width = q.shape
    wide = 64 * GROUP
    steps = width // wide
    head = pl.BlockSpec((1, span, wide), lambda g: (row, 0, g))
    col_t = pl.BlockSpec((wide, span), lambda g: (g, row))
    weight = pl.BlockSpec((width, wide), lambda g: (0, g))
    return pl.pallas_call(
        attn_back_kernel,
        grid=(steps,),
        in_specs=[
            head,
            head,
            head,
            pl.BlockSpec((1, GROUP, span, span), lambda g: (row, g, 0, 0)),
            pl.BlockSpec((1, 1, 8, span), lambda g: (row, g, 0, 0)),
            col_t,
            pl.BlockSpec((wide, span), lambda g: (g, 0)),
            weight,
            weight,
            weight,
            once((span, width)),
        ],
        out_specs=[
            once((cycle, span // cycle, width)),
            pl.BlockSpec((3, span, wide), lambda g: (0, 0, g)),
            pl.BlockSpec((8, wide), lambda g: (0, g)),
        ],
        out_shape=[
            jax.ShapeDtypeStruct((cycle, span // cycle, width), BF16),
            jax.ShapeDtypeStruct((3, span, width), BF16),
            jax.ShapeDtypeStruct((8, width), F32),
        ],
        scratch_shapes=[pltpu.VMEM((span, width), F32), pltpu.VMEM((wide, span), F32)],
        compiler_params=params(),
        cost_estimate=cost(17e9),
        name="attn_back",
    )(q, k, v, e, inv, mix_t, d_mix_t, w_query, w_key, w_value, d_res)


def attn_grad_kernel(part, my_ref, x_t, back0, back1, vec, keep, send, tile_s):
    my = my_ref[0]
    w = pl.program_id(0)
    span = back0.shape[1]
    tile_s[...] = (dot(x_t[:, :span], back0[0]) + dot(x_t[:, span:], back1[0])).astype(BF16)

    def put(ref, at, value):
        ref[at, pl.ds(pl.multiple_of(w * part, 16), part), :] = value

    place_parts(tile_s, my, keep, send, part, put)

    @pl.when(w == 0)
    def _():
        low = vec[...].astype(BF16)
        for p in range(keep.shape[0]):
            keep[p, 3 * part :, :] = low
            send[p, 3 * part :, :] = low


def attn_grads_split(my, x_t, back, vec, groups):
    width, all_tokens = x_t.shape
    part = width // groups
    shape = (groups // 2, 3 * part + 32, width)
    return pl.pallas_call(
        functools.partial(attn_grad_kernel, part),
        grid=(3,),
        in_specs=[
            SMEM,
            once((width, all_tokens)),
            pl.BlockSpec((1, all_tokens // 2, width), lambda w: (w, 0, 0)),
            pl.BlockSpec((1, all_tokens // 2, width), lambda w: (w, 0, 0)),
            once(vec.shape),
        ],
        out_specs=[once(shape)] * 2,
        out_shape=[jax.ShapeDtypeStruct(shape, BF16)] * 2,
        scratch_shapes=[pltpu.VMEM((width, width), BF16)],
        compiler_params=params(),
        cost_estimate=cost(9.5e9),
        name="attn_grads",
    )(my.reshape(1), x_t, *back, vec)


def swap(values, axis, mask):
    size = lax.axis_size(axis)
    return lax.ppermute(values, axis, [(i, i ^ mask) for i in range(size)])


def added(left, right):
    return (left.astype(F32) + right.astype(F32)).astype(BF16)


def exchange(values, axis, groups=None):
    return lax.all_to_all(values, axis, 0, 0, tiled=True, axis_index_groups=groups)


def by_core(blocks):
    turned = jnp.take(blocks, jnp.arange(blocks.shape[0]) ^ lax.axis_index("dp"), axis=0)
    return turned[0::2], turned[1::2]


class ChipSum:
    def __init__(self, keep, send):
        bits = list(range(1, lax.axis_size("dp").bit_length() - 1))
        got = swap(send, "dp", 1)
        half = keep.shape[1] // 2
        alive = list(range(keep.shape[0]))
        self.parts = [
            (keep[:, :half], got[:, :half], alive, bits),
            (keep[:, half:], got[:, half:], alive, bits[::-1]),
        ]

    def advance(self):
        ready, parts = [], []
        for keep, got, alive, bits in self.parts:
            held = added(keep, got)
            if bits:
                bit = bits[0] - 1
                stay = [n for n, p in enumerate(alive) if not (p >> bit) & 1]
                go = [n for n, p in enumerate(alive) if (p >> bit) & 1]
                keep = jnp.stack([held[n] for n in stay])
                send = jnp.stack([held[n] for n in go])
                ready += [keep, send]
                got = swap(send, "dp", 2 << bit)
                parts.append((keep, got, [alive[n] for n in stay], bits[1:]))
            else:
                ready.append(held)
                parts.append(held[0])
        self.parts = parts
        return ready

    def finish(self):
        while isinstance(self.parts[0], tuple):
            self.advance()
        return jnp.concatenate(self.parts, axis=0)


class LineSum:
    def __init__(self, rows):
        place = lax.axis_index("blk")
        size = lax.axis_size("blk")
        self.bits = [1 << b for b in range(size.bit_length() - 1)]
        self.held = rows
        self.mine = [(place // bit) % 2 for bit in self.bits]
        self.step = 0

    def start(self):
        held = self.held.reshape((2, -1) + self.held.shape[1:])
        mine = self.mine[self.step]
        self.keep = lax.dynamic_index_in_dim(held, mine, 0, keepdims=False)
        send = lax.dynamic_index_in_dim(held, 1 - mine, 0, keepdims=False)
        self.got = swap(send, "blk", self.bits[self.step])
        self.step += 1
        return self.keep, send

    def add(self):
        self.held = added(self.keep, self.got)
        return self.held

    def gather(self):
        pieces = self.held[None]
        for bit in self.bits[::-1]:
            pieces = jnp.concatenate([pieces, swap(pieces, "blk", bit)], axis=0)
        return pieces

    def finish(self):
        while self.step < len(self.bits):
            self.start()
            self.add()
        return self.gather()


def row_of(place, piece):
    return (((place % 2) ^ (piece // 2)) * 2) + (((place // 2) % 2) ^ (piece % 2))


def line_join(pieces):
    place = lax.axis_index("blk")
    order = row_of(place, jnp.arange(pieces.shape[0]))
    return jnp.take(pieces, jnp.argsort(order), axis=0).reshape((-1,) + pieces.shape[2:])


def join(place, pieces, rows_ref):
    share = pieces.shape[1]
    for n in range(pieces.shape[0]):
        at = pl.ds(pl.multiple_of(row_of(place, n) * share, 8), share)
        rows_ref[at, :] = pieces[n].astype(F32)


def outer_result_kernel(place_ref, pieces, out, rows_s):
    join(place_ref[0], pieces, rows_s)
    out[...] = rows_s[...].T


def outer_result(place, pieces):
    rows, half = pieces.shape[0] * pieces.shape[1], pieces.shape[2]
    vmem = pl.BlockSpec(memory_space=pltpu.VMEM)
    return pl.pallas_call(
        outer_result_kernel,
        in_specs=[SMEM, vmem],
        out_specs=vmem,
        out_shape=jax.ShapeDtypeStruct((half, rows), F32),
        scratch_shapes=[pltpu.VMEM((rows, half), F32)],
        compiler_params=params(),
        cost_estimate=cost(2e9),
        name="outer_result",
    )(place.reshape(1), pieces)


def inner_result_kernel(place_ref, pieces, inner_out, attn_out, rows_s):
    join(place_ref[0], pieces, rows_s)
    part, wide = inner_out.shape
    width = rows_s.shape[1]
    count = wide // width
    for i in range(count):
        inner_out[:, i * width : (i + 1) * width] = rows_s[i * part : (i + 1) * part, :]
    attn_out[...] = rows_s[count * part :, :]


def inner_result(place, pieces, part):
    rows, width = pieces.shape[0] * pieces.shape[1], pieces.shape[2]
    vmem = pl.BlockSpec(memory_space=pltpu.VMEM)
    return pl.pallas_call(
        inner_result_kernel,
        in_specs=[SMEM, vmem],
        out_specs=[vmem] * 2,
        out_shape=[
            jax.ShapeDtypeStruct((part, (rows // part - 1) * width), F32),
            jax.ShapeDtypeStruct((part, width), F32),
        ],
        scratch_shapes=[pltpu.VMEM((rows, width), F32)],
        compiler_params=params(),
        cost_estimate=cost(2e9),
        name="inner_result",
    )(place.reshape(1), pieces)


def late_kernel(lanes_ref, pieces, *outs):
    late = outs[-1]
    join(lanes_ref[3], pieces, late)
    part = outs[0].shape[0]
    for w in range(3):
        outs[w][...] = late[w * part : (w + 1) * part, :]
    vec = late[3 * part :, :].astype(BF16)
    width = vec.shape[1]
    size = outs[3].shape[1]

    def picked(start, count):
        lanes = -(-count // LANES) * LANES
        source = lax.broadcasted_iota(jnp.int32, (width, lanes), 0)
        target = lax.broadcasted_iota(jnp.int32, (width, lanes), 1)
        return jnp.where(source == target + start, 1.0, 0.0).astype(BF16)

    narrow = dot(vec, picked(lanes_ref[0], size))
    for n in range(8):
        outs[3 + n][...] = narrow[n : n + 1, :size]
    count = outs[11].shape[1]
    broad = dot(vec, picked(lanes_ref[1], count))
    row = lax.broadcasted_iota(jnp.int32, broad.shape, 0)
    broad = jnp.where(row == lanes_ref[2], broad, 0.0)
    outs[11][...] = total(broad)[:, :count]


def late_results(place, pieces, groups, inner_width):
    rows, width = pieces.shape[0] * pieces.shape[1], pieces.shape[2]
    part = (rows - 32) // 3
    size = width // groups
    count = inner_width // groups
    my = lax.axis_index("dp")
    start = my * count
    lanes = jnp.stack([my * size, start % width, 8 + start // width, place]).astype(jnp.int32)
    vmem = pl.BlockSpec(memory_space=pltpu.VMEM)
    shapes = (
        [jax.ShapeDtypeStruct((part, width), F32)] * 3
        + [jax.ShapeDtypeStruct((1, size), F32)] * 8
        + [jax.ShapeDtypeStruct((1, count), F32)]
    )
    outs = pl.pallas_call(
        late_kernel,
        in_specs=[SMEM, vmem],
        out_specs=[vmem] * len(shapes),
        out_shape=shapes,
        scratch_shapes=[pltpu.VMEM((rows, width), F32)],
        compiler_params=params(),
        cost_estimate=cost(3e9),
        name="late_results",
    )(lanes, pieces)
    return list(outs[:3]), [value.reshape(-1) for value in outs[3:]]


def spread_kernel(*refs):
    out = refs[-1]
    for r, piece in enumerate(refs[:-1]):
        out[:, r] = piece[...].astype(out.dtype)


def spread(pieces, dtype):
    micro, blk_len, width = pieces[0].shape
    rows = len(pieces)
    return pl.pallas_call(
        spread_kernel,
        grid=(micro,),
        in_specs=[pl.BlockSpec((1, blk_len, width), lambda m: (m, 0, 0))] * rows,
        out_specs=pl.BlockSpec((1, rows, blk_len, width), lambda m: (m, 0, 0, 0)),
        out_shape=jax.ShapeDtypeStruct((micro, rows, blk_len, width), dtype),
        compiler_params=params(),
        cost_estimate=cost(3e9),
        name="spread",
    )(*pieces)


def local(
    hidden_in,
    seq_lengths,
    dam_mask,
    w_query,
    b_query,
    w_key,
    w_value,
    b_value,
    w_attn_out,
    b_attn_out,
    gain_attn,
    shift_attn,
    w_inner,
    b_inner,
    w_outer,
    b_outer,
    gain_ffn,
    shift_ffn,
    grad_out,
):
    micro, rows, blk_len, width = hidden_in.shape
    cycle = lax.axis_size("blk")
    groups = lax.axis_size("dp")
    inner_width = w_inner.shape[1]
    place = lax.axis_index("blk")
    my = lax.axis_index("dp")

    def whole_row(values, row):
        return exchange(values[:, row], "blk").reshape(-1, width)

    def home(values):
        return exchange(values.reshape(cycle, blk_len, width), "blk")

    def flat(vector):
        return vector.reshape(1, -1)

    x = exchange(hidden_in, "blk")
    lengths = lax.dynamic_index_in_dim(seq_lengths, place, 0, keepdims=False)
    bias = mask_bias(lengths, dam_mask)
    vectors = [
        flat(v)
        for v in (b_attn_out, gain_attn, shift_attn, b_inner, b_outer, gain_ffn, shift_ffn)
    ]
    q, k, v, e, inv, mixed, x_rows, mix_t, x_t = attn_forward(
        x, w_query, w_key, w_value, flat(b_query), flat(b_value), bias
    )
    grads = [whole_row(after(grad_out, x if r == 0 else q), r) for r in range(rows)]
    vec = jnp.zeros((8, width), F32)
    wide = jnp.zeros((8, inner_width), F32)
    kept = []
    results = []
    for r in range(rows):
        result = ffn_both(
            r, grads[r], x_rows, mixed, (w_attn_out, w_inner, w_outer), vectors, vec, wide
        )
        results.append(home(result[0]))
        vec, wide = result[-2:]
        kept.append((None, result[1:-2]))
    hidden_out = spread(results, BF16)

    first_t = [k[1][0] for k in kept]
    hidden = [k[1][1] for k in kept]
    d_inner = [k[1][2] for k in kept]
    d_outer_t = [k[1][3] for k in kept]
    d_attn = [k[1][4] for k in kept]
    part = width // groups
    aligned = part % 16 == 0 and groups == 2 * (inner_width // width)
    if aligned:
        hidden = [after(hidden[0], results[0])] + hidden[1:]
        outer = outer_grads(my, d_outer_t, hidden)
        d_inner = [after(d_inner[0], outer)] + d_inner[1:]
        inner = inner_grads(my, first_t, d_inner, mix_t, d_attn, groups)
    else:
        outer = pair_product(d_outer_t, hidden)
        outer = by_core(outer.reshape(width, groups, -1).transpose(1, 2, 0))
        inner = pair_product(first_t, d_inner).reshape(groups, part, inner_width)
        attn = pair_product(jnp.split(mix_t, rows, axis=1), d_attn).reshape(groups, part, width)
        pieces = jnp.split(inner, inner_width // width, axis=2) + [attn]
        inner = by_core(jnp.concatenate(pieces, axis=1))
    inner = [value.reshape(value.shape[0], -1, width) for value in inner]
    outer_sum = ChipSum(*outer)
    inner_sum = ChipSum(*inner)
    ready = (results[1:], inner, outer_sum.advance())

    vec_two = jnp.zeros((8, width), F32)
    back = []
    returned = []
    for r in range(rows):
        d_res, d_mix_t = kept[r][1][5:7]
        d_res = after(d_res, ready)
        d_row, three, sums = attn_back(
            r, q, k, v, e, inv, mix_t, d_mix_t, w_query, w_key, w_value, d_res, cycle
        )
        returned.append(exchange(d_row, "blk"))
        vec_two = vec_two + sums
        back.append(three)
        if r == 0:
            ready = (outer_sum.advance(), inner_sum.advance())

    small = jnp.concatenate(
        [vec_two[:2], vec[:6], wide[0].reshape(-1, width), jnp.zeros((20, width), F32)], axis=0
    )
    small = after(small, returned[0], outer_sum.advance(), inner_sum.advance())
    outer_line = LineSum(outer_sum.finish())
    outer_line.start()
    if aligned:
        late = attn_grads_split(my, x_t, back, small, groups)
    else:
        halves = jnp.split(x_t, rows, axis=1)
        late = [pair_product(halves, [b[w] for b in back]) for w in range(3)]
        late = [value.reshape(groups, part, width) for value in late]
        late.append(jnp.broadcast_to(small.astype(BF16), (groups, 32, width)))
        late = by_core(jnp.concatenate(late, axis=1))
    late_sum = ChipSum(*late)
    grad_in = spread(returned, F32)
    outer_line.add()
    outer = outer_line.finish()
    inner = LineSum(inner_sum.finish()).finish()
    late = LineSum(late_sum.finish()).finish()
    if aligned:
        g_outer = outer_result(place, outer)
        g_inner, g_attn = inner_result(place, inner, part)
        mats, vecs = late_results(place, late, groups, inner_width)
    else:
        g_outer = line_join(outer).astype(F32)
        inner = line_join(inner).astype(F32)
        late = line_join(late)
        g_inner = jnp.concatenate(
            [inner[i * part : (i + 1) * part] for i in range(inner_width // width)], axis=1
        )
        g_attn = inner[part * (inner_width // width) :]
        mats = [late[w * part : (w + 1) * part].astype(F32) for w in range(3)]
        sums = late[3 * part :].astype(F32)
        vecs = [
            lax.dynamic_slice_in_dim(sums[n], my * part, part, 0) for n in range(8)
        ]
        count = inner_width // groups
        vecs.append(lax.dynamic_slice_in_dim(sums[8:12].reshape(-1), my * count, count, 0))
    g_query, g_key, g_value = mats
    s_query, s_value, s_attn, s_gain, s_shift, s_outer, s_gain2, s_shift2, s_inner = vecs
    return (
        hidden_out,
        grad_in,
        g_query,
        s_query,
        g_key,
        g_value,
        s_value,
        g_attn,
        s_attn,
        s_gain,
        s_shift,
        g_inner,
        s_inner,
        g_outer,
        s_outer,
        s_gain2,
        s_shift2,
    )


def solution(mesh):
    placed = (P(None, "dp", "blk", None), P(None, "dp", None)) + (P(),) * 16
    placed = placed + (P(None, "dp", "blk", None),)
    return jax.shard_map(
        local,
        mesh=mesh,
        in_specs=placed,
        out_specs=(
            P(None, "dp", "blk", None),
            P(None, "dp", "blk", None),
            P("dp", None),
            P("dp"),
            P("dp", None),
            P("dp", None),
            P("dp"),
            P("dp", None),
            P("dp"),
            P("dp"),
            P("dp"),
            P("dp", None),
            P("dp"),
            P("dp", None),
            P("dp"),
            P("dp"),
            P("dp"),
        ),
        check_vma=False,
    )
```
